32 devices in a mesh: stream: 4 (over z), span: 8 (over y, x, core).
Axes of the slice: x: 2, y: 2, z: 4, core: 2. Of those that a mesh axis runs over, the one named last changes fastest.
Arguments:
- velocity: float32 [3, 32, 128, 1024], P(None, 'stream', 'span'), may hold values from -36 to 36
- coefficient: float32 [32, 128, 1024], P('stream', 'span'), may hold values from 0.5 to 4
- coords: float32 [3, 4096], P(None, ('stream', 'span')), may hold values from -1 to 1
- forces: float32 [3, 4096], P(None, ('stream', 'span')), may hold values from -12 to 12
- line_id: int32 [4096], P(('stream', 'span')), may hold values from 0 to 399
- line_gain: float32 [400], replicated, may hold values from 0.5 to 2
- dest_span: int32 [4096, 1], P(('stream', 'span')), may hold values from 0 to 7; in each aligned block of 128 rows (0 to 127, 128 to 255, ...) at most 32 rows name the same one
- owner_element: int32 [4096], P(('stream', 'span')), may hold values from 0 to 255
Outputs:
- pressure: float32 [32, 128, 1024], P('stream', 'span')
- residual: float32 [32, 128, 1024], P('stream', 'span')
The draws below stay inside these ranges and needn't reach their ends.
Inputs may be any that keep to these rules, and one draw needn't show every extreme that they name: `dest_span`: of the 128 blade points of one device, at most 32 name the same span index, and in every draw some span index is named by exactly 32 of one device's points. `owner_element`: an element of the device at the point's span index in the same slab, numbered (ex * 2 + ey) * 128 + ez.
All inputs are finite; a program needn't handle non-finite values.
Results may differ from the reference program's by a relative error of at most 0.00019.
Values sent between devices are 32-bit elements; how exact they have to be, the bound alone decides.
A program may use at most 64 MiB of HBM per device.

```python
import math
import jax
import jax.numpy as jnp
import numpy as np
from jax import lax

POLY = 8
EX = 1
EY = 2
EZ = 128
PTS_DEV = 128
LINES = 400
ITERS = 3
CAP = 32
SLAB_PTS = 1024
POINTS = 4096
GX = 32
GY = 128
GZ = 1024
N_SPAN = 8


def draw_velocity(key, part):
    stream_frac = jnp.arange(GX, dtype=jnp.float32) / GX
    span_frac = jnp.arange(GY, dtype=jnp.float32) / GY
    amplitude = 0.3 * (1.0 + 2.0 * stream_frac)[:, None] * (10.0 ** span_frac)[None, :]
    noise_field = jnp.clip(jax.random.normal(key, (3, GX, GY, GZ), jnp.float32), -4.0, 4.0)
    return noise_field * amplitude[None, :, :, None]


def with_ends(array, stream_key, least, top_value):
    shape = array.shape
    index_at = [jax.random.randint(jax.random.fold_in(stream_key, axis), (), 0, shape[axis]) for axis in range(len(shape))]
    array = array.at[tuple(index_at)].set(least)
    longest = shape.index(max(shape))
    index_at[longest] = (index_at[longest] + 1) % shape[longest]
    return array.at[tuple(index_at)].set(top_value)


def block_scale(own_key, dims, cuts, low, top_value):
    gain, own = 1.0, jax.random.fold_in(own_key, 6)
    for dim, parts in cuts:
        draws = jnp.exp(jax.random.uniform(jax.random.fold_in(own, dim), (parts,), jnp.float32, low / len(cuts), top_value / len(cuts)))
        gain = gain * jnp.repeat(draws, dims[dim] // parts).reshape([-1 if axis == dim else 1 for axis in range(len(dims))])
    return gain


def routed_block(stream_key, own, number, rows, amount, top, limit, skew):
    order = jax.random.permutation(stream_key, amount)
    crowded, usual = load_shares(amount, rows * top, limit, skew, True), load_shares(amount, rows * top, limit, skew, False)
    places = jnp.arange(amount)

    def named(lengths, offset_by):
        used = int((lengths > 0).sum())
        fixed = max(1, used // 4)
        moved = fixed + (places - fixed + offset_by * (used - fixed)) % max(1, amount - fixed)
        return jnp.zeros((amount,), jnp.int32).at[order[jnp.where(places < fixed, places, moved)]].set(jnp.asarray(lengths, jnp.int32))

    lengths = jnp.where(number % 4 == 0, named(crowded, number // 4), named(usual, number - number // 4 - 1))
    mixed = jax.random.permutation(jax.random.fold_in(own, 3), amount)
    giver, sink = mixed[0:amount // 2 * 2:2], mixed[1:amount // 2 * 2:2]
    margin = jnp.minimum(lengths[giver] - 1, limit - lengths[sink]) // 2
    margin = jnp.where((giver == order[0]) | (sink == order[0]) | (lengths[sink] == 0), 0, jnp.maximum(margin, 0))
    moved = jax.random.randint(jax.random.fold_in(own, 4), (amount // 2,), 0, 1 << 20) % (margin + 1)
    lengths = lengths.at[giver].add(-moved).at[sink].add(moved)
    items = jnp.searchsorted(jnp.cumsum(lengths), jnp.arange(rows * top), side="right").astype(jnp.int32)
    table = items.reshape(top, rows).T
    table = table[jax.random.permutation(jax.random.fold_in(own, 1), rows)]
    offset_by = jax.random.randint(jax.random.fold_in(own, 2), (rows, 1), 0, top)
    return jnp.take_along_axis(table, (jnp.arange(top)[None, :] + offset_by) % top, axis=1)


def load_shares(number_of, total, most, slope, full):
    weights = [(1 << 20) // math.isqrt(standing ** slope) + 1 for standing in range(1, number_of + 1)]
    largest = most if full else min(most, max(-(-total // number_of), total * weights[0] // sum(weights)))
    least = 1 if total - largest >= number_of - 1 else 0
    holding, spare = [largest] + [least] * (number_of - 1), total - largest - least * (number_of - 1)
    while spare > 0:
        free = [i for i in range(1, number_of) if holding[i] < largest] or [i for i in range(1, number_of) if holding[i] < most]
        mass, remaining = sum([weights[i] for i in free]), spare
        for i in free:
            more = min(most - holding[i], max(1, remaining * weights[i] // mass), spare)
            holding[i] = holding[i] + more
            spare = spare - more
    return np.array(holding)


def noise(stream_key, shape, deviation, most, cuts=(), kind=jnp.bfloat16):
    level = block_scale(stream_key, shape, cuts, -0.22, 0.18) if cuts else 1.0
    values = jax.random.normal(stream_key, shape, jnp.float32) * deviation * level
    return jnp.minimum(jnp.maximum(values, -most), most).astype(kind)


def setup_inputs(seed: int = 0) -> dict:
    splits = jax.random.split(jax.random.key(seed), 9)
    velocity = draw_velocity(jax.random.fold_in(splits[8], 71), 0)
    coefficient = jnp.clip(jnp.exp(math.log(4.0) - 2.0794415 * jax.random.uniform(splits[1], (GX, GY, GZ), jnp.float32) ** block_scale(splits[1], (GX, GY, GZ), ((0, 4), (1, 8)), -0.2, 0.2)), 0.5, 4.0)
    coords = jnp.clip(jax.random.uniform(splits[2], (3, POINTS), jnp.float32, -1.0, 1.0) * block_scale(splits[2], (3, POINTS), ((1, 32),), -0.4, 0.0), -1.0, 1.0)
    forces = noise(splits[3], (3, POINTS), 3.0, 12.0, ((1, 32),), jnp.float32)
    line_id = with_ends(jax.random.randint(splits[4], (POINTS,), 0, LINES), jax.random.fold_in(splits[4], 1), 0, LINES - 1).astype(jnp.int32)
    line_gain = jnp.clip(jnp.exp(jax.random.uniform(splits[5], (LINES,), jnp.float32, math.log(0.5), math.log(2.0))), 0.5, 2.0)
    dest_span_keys = jax.random.split(jax.random.fold_in(splits[6], 1), POINTS // PTS_DEV)
    dest_span_turns = jax.random.permutation(jax.random.fold_in(splits[6], 3), POINTS // PTS_DEV)
    dest_span = jax.vmap(lambda own, number: routed_block(jax.random.fold_in(splits[6], 2), own, number, PTS_DEV, N_SPAN, 1, CAP, 2))(dest_span_keys, dest_span_turns).reshape((POINTS, 1))
    owner_element = with_ends(jax.random.randint(splits[7], (POINTS,), 0, EX * EY * EZ), jax.random.fold_in(splits[7], 1), 0, (EX * EY * EZ) - 1).astype(jnp.int32)
    return {"velocity": velocity, "coefficient": coefficient, "coords": coords, "forces": forces, "line_id": line_id, "line_gain": line_gain, "dest_span": dest_span, "owner_element": owner_element}


kernel_width = 0.45
gll_nodes = [-1.0, -0.8717401485096066, -0.5917001814331423, -0.2092992179024789,
             0.2092992179024789, 0.5917001814331423, 0.8717401485096066, 1.0]


def legendre_value(point, degree):
    previous = 1.0
    current = point
    for order in range(1, degree):
        following = ((2 * order + 1) * point * current - order * previous) / (order + 1)
        previous = current
        current = following
    return current


def gll_tables():
    degree = POLY - 1
    values = [legendre_value(point, degree) for point in gll_nodes]
    weights = [2.0 / (degree * (degree + 1) * value * value) for value in values]
    diffmat = []
    for row_at in range(POLY):
        row_list = []
        for col_at in range(POLY):
            if row_at != col_at:
                row_list.append(values[row_at] / (values[col_at] * (gll_nodes[row_at] - gll_nodes[col_at])))
            elif row_at == 0:
                row_list.append(-degree * (degree + 1) / 4.0)
            elif row_at == degree:
                row_list.append(degree * (degree + 1) / 4.0)
            else:
                row_list.append(0.0)
        diffmat.append(row_list)
    return (jnp.asarray(gll_nodes, dtype=jnp.float32), jnp.asarray(weights, dtype=jnp.float32),
            jnp.asarray(diffmat, dtype=jnp.float32))


def derive(grid_field, diffmat, axis_at, flipped):
    matrix = diffmat.T if flipped else diffmat
    extent0, extent1, extent2 = grid_field.shape
    highest = lax.Precision.HIGHEST
    if axis_at == 0:
        blocks = grid_field.reshape(extent0 // POLY, POLY, extent1, extent2)
        result = jnp.einsum("ia,xayz->xiyz", matrix, blocks, precision=highest)
    elif axis_at == 1:
        blocks = grid_field.reshape(extent0, extent1 // POLY, POLY, extent2)
        result = jnp.einsum("ib,xybz->xyiz", matrix, blocks, precision=highest)
    else:
        blocks = grid_field.reshape(extent0, extent1, extent2 // POLY, POLY)
        result = jnp.einsum("xyzc,ic->xyzi", blocks, matrix, precision=highest)
    return result.reshape(grid_field.shape)


def along_axis(vector, axis_at):
    shape_at = [1, 1, 1]
    shape_at[axis_at] = vector.shape[0]
    return vector.reshape(shape_at)


def assemble(grid_field):
    running = grid_field
    nothing = jnp.zeros_like(grid_field)
    for axis_at in range(3):
        extent = running.shape[axis_at]
        node = lax.iota(jnp.int32, extent) % POLY
        first = along_axis(node == 0, axis_at)
        last = along_axis(node == POLY - 1, axis_at)
        widths = [(0, 0), (0, 0), (0, 0)]
        widths[axis_at] = (1, 1)
        padded = jnp.pad(running, widths)
        before = lax.slice_in_dim(padded, 0, extent, axis=axis_at)
        after = lax.slice_in_dim(padded, 2, extent + 2, axis=axis_at)
        running = running + jnp.where(first, before, nothing) + jnp.where(last, after, nothing)
    return running


def inverse_multiplicity(extent):
    node = lax.iota(jnp.int32, extent) % POLY
    position = lax.iota(jnp.int32, extent)
    inner_face = ((node == 0) & (position > 0)) | ((node == POLY - 1) & (position < extent - 1))
    return jnp.where(inner_face, 0.5, 1.0).astype(jnp.float32)


def apply_operator(grid_field, weight3, metric, diffmat):
    running = weight3 * grid_field
    for axis_at in range(3):
        running = running + derive(metric * derive(grid_field, diffmat, axis_at, False), diffmat, axis_at, True)
    return assemble(running)


def reference(velocity, coefficient, coords, forces, line_id, line_gain, dest_span, owner_element):
    abscissa, weights, diffmat = gll_tables()
    extent0, extent1, extent2 = coefficient.shape
    tile_zero = jnp.tile(weights, extent0 // POLY)
    tile_one = jnp.tile(weights, extent1 // POLY)
    tile_two = jnp.tile(weights, extent2 // POLY)
    weight3 = (tile_zero[:, None, None] * tile_one[None, :, None]) * tile_two[None, None, :]
    metric = weight3 * coefficient
    inv_mult = (inverse_multiplicity(extent0)[:, None, None] * inverse_multiplicity(extent1)[None, :, None]) * inverse_multiplicity(extent2)[None, None, :]

    gains = line_gain[line_id]
    scaled = forces * gains[None, :]
    kernels = []
    for dimension in range(3):
        kernels.append(jnp.exp(-(((abscissa[None, :] - coords[dimension][:, None]) / kernel_width) ** 2)))
    kernel3 = (kernels[0][:, :, None, None] * kernels[1][:, None, :, None]) * kernels[2][:, None, None, :]
    contrib = scaled.T[:, :, None, None, None] * kernel3[:, None]
    point_at = jnp.arange(coords.shape[1], dtype=jnp.int32)
    slab = point_at // SLAB_PTS
    target = dest_span[:, 0]
    elem_x = slab * EX + owner_element // (EY * EZ)
    elem_y = target * EY + (owner_element // EZ) % EY
    elem_z = owner_element % EZ
    elem_view = jnp.zeros((extent0 // POLY, extent1 // POLY, extent2 // POLY, 3, POLY, POLY, POLY), jnp.float32)
    elem_view = elem_view.at[elem_x, elem_y, elem_z].add(contrib)
    forcing = elem_view.transpose(3, 0, 4, 1, 5, 2, 6).reshape(3, extent0, extent1, extent2)

    running = derive(weight3 * (velocity[0] + forcing[0]), diffmat, 0, True)
    running = running + derive(weight3 * (velocity[1] + forcing[1]), diffmat, 1, True)
    running = running + derive(weight3 * (velocity[2] + forcing[2]), diffmat, 2, True)
    rhs = assemble(running)

    def weighted(first_vec, second_vec):
        return jnp.sum(first_vec * second_vec * inv_mult)

    pressure = jnp.zeros_like(rhs)
    residual = rhs
    direction = rhs
    norm_now = weighted(residual, residual)
    for iteration in range(ITERS):
        applied = apply_operator(direction, weight3, metric, diffmat)
        step_len = norm_now / weighted(direction, applied)
        pressure = pressure + step_len * direction
        residual = residual - step_len * applied
        norm_next = weighted(residual, residual)
        direction = residual + (norm_next / norm_now) * direction
        norm_now = norm_next
    return pressure, residual
```

```python
import functools

import jax
import jax.numpy as jnp
import numpy as np
from jax import lax
from jax.experimental import pallas as pl
from jax.experimental.pallas import tpu as pltpu
from jax.sharding import PartitionSpec as P

POLY = 8
ITERS = 3
LANES = 128
CHUNK = 256

kernel_width = 0.45
gll_nodes = [
    -1.0,
    -0.8717401485096066,
    -0.5917001814331423,
    -0.2092992179024789,
    0.2092992179024789,
    0.5917001814331423,
    0.8717401485096066,
    1.0,
]
MESH = pl.DeviceIdType.MESH
PAIRS = [(0, 0), (0, 1), (1, 1), (0, 2), (1, 2), (2, 2), (0, 3), (1, 3), (2, 3)]
OFFSETS = [(1, 0), (-1, 0), (0, 1), (0, -1), (1, 1), (1, -1), (-1, 1), (-1, -1)]


def legendre_value(point, degree):
    previous = 1.0
    current = point
    for order in range(1, degree):
        following = ((2 * order + 1) * point * current - order * previous) / (order + 1)
        previous = current
        current = following
    return current


def gll_tables():
    degree = POLY - 1
    values = [legendre_value(point, degree) for point in gll_nodes]
    weights = [2.0 / (degree * (degree + 1) * value * value) for value in values]
    diffmat = np.zeros((POLY, POLY))
    for i in range(POLY):
        for j in range(POLY):
            if i != j:
                diffmat[i, j] = values[i] / (values[j] * (gll_nodes[i] - gll_nodes[j]))
    diffmat[0, 0] = -degree * (degree + 1) / 4.0
    diffmat[-1, -1] = degree * (degree + 1) / 4.0
    return (
        np.asarray(gll_nodes, np.float32),
        np.asarray(weights, np.float32),
        np.asarray(diffmat, np.float32),
    )


def split_np(matrix):
    high = matrix.astype(jnp.bfloat16)
    low = (matrix - high.astype(np.float32)).astype(jnp.bfloat16)
    return high, low


def constants(extent0, extent1):
    nodes, weights, diffmat = gll_tables()
    eye = functools.partial(np.eye, dtype=np.float32)
    along0 = np.kron(eye(extent0 // POLY), np.kron(diffmat, eye(extent1)))
    along1 = np.kron(eye(extent0 * extent1 // POLY), diffmat)
    rows = np.concatenate([along0, along1], axis=0)
    cols = np.kron(eye(CHUNK // POLY), diffmat)

    def left(matrix):
        high, low = split_np(matrix)
        return np.concatenate([high, high, low], axis=1)

    def right(matrix):
        high, low = split_np(matrix)
        return np.concatenate([high, high, low], axis=0)

    row_weight = np.kron(np.tile(weights, extent0 // POLY), np.tile(weights, extent1 // POLY))
    row_weight = row_weight.astype(np.float32)
    weight = row_weight[:, None] * np.tile(weights, CHUNK // POLY)[None, :]
    column = np.repeat(nodes[:, None], LANES, axis=1)
    return left(rows), left(rows.T.copy()), right(cols.T.copy()), right(cols), weight, column


def split2(value):
    high = value.astype(jnp.bfloat16)
    low = (value - high.astype(jnp.float32)).astype(jnp.bfloat16)
    return high, low


def split3(value):
    high = value.astype(jnp.bfloat16)
    rest = value - high.astype(jnp.float32)
    middle = rest.astype(jnp.bfloat16)
    low = (rest - middle.astype(jnp.float32)).astype(jnp.bfloat16)
    return high, middle, low


def dot(first, second):
    return jnp.dot(first, second, preferred_element_type=jnp.float32)


def dot_nt(first, second):
    return lax.dot_general(
        first, second, (((1,), (1,)), ((), ())), preferred_element_type=jnp.float32
    )


def stacked(value, axis):
    high, low = split2(value)
    return jnp.concatenate([high, low, high], axis=axis)


def combine(first, second, gram):
    total = 0.0
    for i, x in enumerate(first):
        for j, y in enumerate(second):
            if x is not None and y is not None:
                total = total + x * y * gram[(min(i, j), max(i, j))]
    return total


def body(
    sizes,
    velocity,
    coefficient,
    coords,
    forces,
    line_id,
    line_gain,
    dest_span,
    owner,
    rows_fwd,
    rows_bwd,
    cols_fwd,
    cols_bwd,
    weight,
    nodes,
    pressure,
    residual,
    vel,
    metric,
    basis,
    work,
    inv_mult,
    out_pts,
    in_pts,
    lhs_pts,
    rhs_pts,
    send_stream,
    recv_stream,
    send_span,
    recv_span,
    send_edge,
    recv_edge,
    sums1,
    sums2,
    load_sem,
    pts_send,
    pts_recv,
    halo_send,
    halo_recv,
    sum1_send,
    sum1_recv,
    sum2_send,
    sum2_recv,
):
    n_stream, n_span, extent0, extent1, extent2, capacity = sizes
    rows = extent0 * extent1
    me_s, me_p = lax.axis_index("stream"), lax.axis_index("span")

    loads = [pltpu.make_async_copy(velocity.at[c], vel.at[c], load_sem.at[c]) for c in range(3)]
    loads.append(pltpu.make_async_copy(coefficient, metric, load_sem.at[3]))
    for load in loads:
        load.start()

    def exists(offset):
        s, p = me_s + offset[0], me_p + offset[1]
        return (s >= 0) & (s < n_stream) & (p >= 0) & (p < n_span)

    def at_offset(offset):
        return (
            lax.rem(me_s + offset[0] + n_stream, n_stream),
            lax.rem(me_p + offset[1] + n_span, n_span),
        )

    span_peers = [lax.rem(me_p + j, n_span) for j in range(1, n_span)]
    stream_peers = [lax.rem(me_s + j, n_stream) for j in range(1, n_stream)]

    barrier = pltpu.get_barrier_semaphore()
    for peer in span_peers:
        pl.semaphore_signal(barrier, inc=1, device_id=(me_s, peer), device_id_type=MESH)
    for peer in stream_peers:
        pl.semaphore_signal(barrier, inc=1, device_id=(peer, me_p), device_id_type=MESH)
    greeted = n_span - 1 + n_stream - 1
    for offset in OFFSETS[4:]:

        @pl.when(exists(offset))
        def _(offset=offset):
            pl.semaphore_signal(
                barrier, inc=1, device_id=at_offset(offset), device_id_type=MESH
            )

        greeted = greeted + exists(offset).astype(jnp.int32)

    points = coords.shape[1]
    group = LANES // capacity
    groups = n_span // group
    lines = line_gain.shape[1]
    ids = line_id[...]
    chosen = (lax.broadcasted_iota(jnp.int32, (lines, points), 0) == ids).astype(jnp.bfloat16)
    gain = sum(dot(part, chosen) for part in reversed(split3(line_gain[...])))
    scaled = forces[...] * gain
    target = dest_span[...]
    spans_at = lax.broadcasted_iota(jnp.int32, (n_span, points), 0)
    named = (spans_at == target).astype(jnp.float32)
    earlier = (
        lax.broadcasted_iota(jnp.int32, (points, points), 0)
        < lax.broadcasted_iota(jnp.int32, (points, points), 1)
    ).astype(jnp.bfloat16)
    before = dot(named.astype(jnp.bfloat16), earlier)
    rank = jnp.sum(named * before, axis=0, keepdims=True).astype(jnp.int32)
    slot = target * LANES + lax.rem(me_p, group) * capacity + rank
    payload = jnp.concatenate(
        [
            coords[...],
            scaled,
            owner[...].astype(jnp.float32),
            jnp.zeros((1, points), jnp.float32),
        ],
        axis=0,
    )
    parts = jnp.concatenate(
        [p.astype(jnp.float32) for p in split3(payload)], axis=0
    ).astype(jnp.bfloat16)
    for dest in range(n_span):
        placed = (
            lax.broadcasted_iota(jnp.int32, (LANES, points), 0) + dest * LANES == slot
        ).astype(jnp.float32).astype(jnp.bfloat16)
        tile = dot_nt(parts, placed)
        out_pts[dest] = (tile[16:24] + tile[8:16]) + tile[0:8]

    pl.semaphore_wait(barrier, greeted)

    def points_copy(peer, slot_at):
        return pltpu.make_async_remote_copy(
            src_ref=out_pts.at[peer],
            dst_ref=in_pts.at[slot_at],
            send_sem=pts_send.at[peer],
            recv_sem=pts_recv.at[slot_at],
            device_id=(me_s, peer),
            device_id_type=MESH,
        )

    for peer in span_peers:
        points_copy(peer, me_p).start()
    in_pts[me_p] = out_pts[me_p]

    row_at = lax.broadcasted_iota(jnp.int32, (rows, LANES), 0)
    lane_at = lax.broadcasted_iota(jnp.int32, (rows, LANES), 1)
    at0, at1 = row_at // extent1, row_at % extent1
    pos0 = me_s * extent0 + at0
    pos1 = me_p * extent1 + at1

    def halves(node, inner):
        face = (node == 0) | (node == POLY - 1)
        return jnp.where(face & inner, 0.5, 1.0).astype(jnp.float32)

    mult = halves(at0 % POLY, (pos0 > 0) & (pos0 < extent0 * n_stream - 1))
    mult = mult * halves(at1 % POLY, (pos1 > 0) & (pos1 < extent1 * n_span - 1))
    for block in range(extent2 // LANES):
        pos2 = block * LANES + lane_at
        here = mult * halves(pos2 % POLY, (pos2 > 0) & (pos2 < extent2 - 1))
        inv_mult[:, block * LANES : (block + 1) * LANES] = here

    chunks = [slice(c, c + CHUNK) for c in range(0, extent2, CHUNK)]
    loads[3].wait()
    for cols in chunks:
        metric[:, cols] = metric[:, cols] * weight[...]

    for peer in span_peers:
        points_copy(peer, peer).wait_recv()

    elems2 = extent2 // POLY
    total_pts = groups * LANES
    arrived = []
    for g in range(groups):
        tile = in_pts[g * group]
        for i in range(1, group):
            tile = tile + in_pts[g * group + i]
        arrived.append(tile)
    node_col = nodes[...]
    for g in range(groups):
        tile = arrived[g]
        lanes = slice(g * LANES, (g + 1) * LANES)
        kern = [
            jnp.exp(-(((node_col - tile[k : k + 1]) / kernel_width) ** 2)) for k in range(3)
        ]
        elem = tile[6:7].astype(jnp.int32)
        elem_y = lax.rem(lax.div(elem, elems2), extent1 // POLY)
        elem_x = lax.div(elem, elems2 * (extent1 // POLY))
        elem_z = lax.rem(elem, elems2)
        for c in range(3):
            for a in range(extent0):
                for ey in range(extent1 // POLY):
                    mine = (elem_x == a // POLY) & (elem_y == ey)
                    factor = jnp.where(mine, tile[3 + c : 4 + c] * kern[0][a % POLY : a % POLY + 1], 0.0)
                    base = c * rows + a * extent1 + ey * POLY
                    lhs_pts[base : base + POLY, lanes] = factor * kern[1]
        for ez in range(elems2):
            rhs_pts[ez * POLY : (ez + 1) * POLY, lanes] = jnp.where(elem_z == ez, kern[2], 0.0)

    left_pts = stacked(lhs_pts[...], 1)

    def rhs_chunk(cols):
        high, low = split2(rhs_pts[cols, :])
        force = dot_nt(left_pts, jnp.concatenate([high, high, low], axis=1))
        part = [weight[...] * (vel[c, :, cols] + force[c * rows : (c + 1) * rows]) for c in range(3)]
        both = jnp.concatenate(part[:2], axis=0)
        work[:, cols] = dot(rows_bwd[...], stacked(both, 0)) + dot(
            stacked(part[2], 1), cols_bwd[...]
        )

    def operator_chunk(k, cols):
        field = basis[k, :, cols]
        high, low = split2(field)
        m = metric[:, cols]
        grad = dot(rows_fwd[...], jnp.concatenate([high, low, high], axis=0))
        grad2 = dot(jnp.concatenate([high, low, high], axis=1), cols_fwd[...])
        both = jnp.concatenate([grad[:rows] * m, grad[rows:] * m], axis=0)
        work[:, cols] = (
            dot(rows_bwd[...], stacked(both, 0))
            + dot(stacked(grad2 * m, 1), cols_bwd[...])
            + weight[...] * field
        )

    last0, last1 = extent0 - 1, extent1 - 1

    def halo_copy(k, d):
        offset = OFFSETS[d]
        if d < 2:
            src, dst = send_stream.at[k, d], recv_stream.at[k, d]
        elif d < 4:
            src, dst = send_span.at[k, d - 2], recv_span.at[k, d - 2]
        else:
            src, dst = send_edge.at[k, d - 4], recv_edge.at[k, d - 4]
        return pltpu.make_async_remote_copy(
            src_ref=src,
            dst_ref=dst,
            send_sem=halo_send.at[k, d],
            recv_sem=halo_recv.at[k, d],
            device_id=at_offset(offset),
            device_id_type=MESH,
        )

    def halo_start(k, d):
        @pl.when(exists(OFFSETS[d]))
        def _():
            halo_copy(k, d).start()

    def from_offset(d):
        return exists((-OFFSETS[d][0], -OFFSETS[d][1]))

    def assemble(k):
        lane = lax.broadcasted_iota(jnp.int32, (POLY, extent2), 1)
        first2 = (lane % POLY == 0) & (lane > 0)
        last2 = (lane % POLY == POLY - 1) & (lane < extent2 - 1)
        sub = lax.broadcasted_iota(jnp.int32, (POLY, extent2), 0)
        order = [0, last0] + list(range(1, last0))
        for a in order:
            tiles = []
            for ey in range(extent1 // POLY):
                base = a * extent1 + ey * POLY
                x = work[base : base + POLY, :]
                lower = pltpu.roll(x, 1, 1)
                upper = pltpu.roll(x, extent2 - 1, 1)
                tiles.append(x + jnp.where(first2, lower, 0.0) + jnp.where(last2, upper, 0.0))
            joined = []
            for ey, x in enumerate(tiles):
                y = x
                if ey > 0:
                    y = y + jnp.where(sub == 0, pltpu.roll(tiles[ey - 1], 1, 0), 0.0)
                if ey + 1 < len(tiles):
                    y = y + jnp.where(
                        sub == POLY - 1, pltpu.roll(tiles[ey + 1], POLY - 1, 0), 0.0
                    )
                joined.append(y)
            for ey, y in enumerate(joined):
                base = a * extent1 + ey * POLY
                basis[k, base : base + POLY, :] = y
                if a == last0:
                    send_stream[k, 0, ey * POLY : (ey + 1) * POLY, :] = y
                if a == 0:
                    send_stream[k, 1, ey * POLY : (ey + 1) * POLY, :] = y
            top, bottom = joined[-1][POLY - 1 : POLY], joined[0][0:1]
            send_span[k, 0, a : a + 1, :] = top
            send_span[k, 1, a : a + 1, :] = bottom
            if a == last0:
                send_edge[k, 0] = top
                send_edge[k, 1] = bottom
                for d in (0, 4, 5):
                    halo_start(k, d)
            if a == 0:
                send_edge[k, 2] = top
                send_edge[k, 3] = bottom
                for d in (1, 6, 7):
                    halo_start(k, d)
        halo_start(k, 2)
        halo_start(k, 3)

        def arrive(d, base, count):
            @pl.when(from_offset(d))
            def _():
                halo_copy(k, d).wait_recv()
                basis[k, base : base + count, :] = (
                    basis[k, base : base + count, :] + recv_stream[k, d]
                )

        def arrive_span(d, at):
            @pl.when(from_offset(d))
            def _():
                halo_copy(k, d).wait_recv()
                for a in range(extent0):
                    row = a * extent1 + at
                    basis[k, row : row + 1, :] = (
                        basis[k, row : row + 1, :] + recv_span[k, d - 2, a : a + 1, :]
                    )

        def arrive_edge(d, row):
            @pl.when(from_offset(d))
            def _():
                halo_copy(k, d).wait_recv()
                basis[k, row : row + 1, :] = basis[k, row : row + 1, :] + recv_edge[k, d - 4]

        arrive_span(2, 0)
        arrive_span(3, last1)
        arrive_edge(4, 0)
        arrive_edge(5, last1)
        arrive_edge(6, last0 * extent1)
        arrive_edge(7, last0 * extent1 + last1)
        arrive(0, 0, extent1)
        arrive(1, last0 * extent1, extent1)

    for load in loads[:3]:
        load.wait()
    for cols in chunks:
        rhs_chunk(cols)
    assemble(0)
    for k in range(ITERS):
        for cols in chunks:
            operator_chunk(k, cols)
        assemble(k + 1)

    def partial(step, totals):
        at = pl.ds(pl.multiple_of(step * POLY, POLY), POLY)
        mult_at = inv_mult[at, :]
        vec = [basis[i, at, :] for i in range(ITERS + 1)]
        scaled_vec = [vec[i] * mult_at for i in range(ITERS)]
        new = []
        for total, (i, j) in zip(totals, PAIRS):
            prod = scaled_vec[i] * vec[j]
            for block in range(extent2 // LANES):
                total = total + prod[:, block * LANES : (block + 1) * LANES]
            new.append(total)
        return tuple(new)

    totals = lax.fori_loop(
        0,
        rows // POLY,
        partial,
        tuple(jnp.zeros((POLY, LANES), jnp.float32) for _ in PAIRS),
    )
    mine = [jnp.sum(total, axis=0, keepdims=True) for total in totals]
    mine.append(jnp.zeros((16 - len(PAIRS), LANES), jnp.float32))
    sums1[me_p] = jnp.concatenate(mine, axis=0)

    def sum1_copy(peer, slot_at):
        return pltpu.make_async_remote_copy(
            src_ref=sums1.at[me_p],
            dst_ref=sums1.at[slot_at],
            send_sem=sum1_send.at[peer],
            recv_sem=sum1_recv.at[slot_at],
            device_id=(me_s, peer),
            device_id_type=MESH,
        )

    def sum2_copy(peer, slot_at):
        return pltpu.make_async_remote_copy(
            src_ref=sums2.at[me_s],
            dst_ref=sums2.at[slot_at],
            send_sem=sum2_send.at[peer],
            recv_sem=sum2_recv.at[slot_at],
            device_id=(peer, me_p),
            device_id_type=MESH,
        )

    for peer in span_peers:
        sum1_copy(peer, me_p).start()
    for peer in span_peers:
        sum1_copy(peer, peer).wait_recv()
    total = sums1[0]
    for i in range(1, n_span):
        total = total + sums1[i]
    sums2[me_s] = total
    for peer in stream_peers:
        sum2_copy(peer, me_s).start()
    for peer in stream_peers:
        sum2_copy(peer, peer).wait_recv()
    total = sums2[0]
    for i in range(1, n_stream):
        total = total + sums2[i]
    total = jnp.broadcast_to(jnp.sum(total, axis=1, keepdims=True), (16, LANES))
    gram = {pair: total[n : n + 1] for n, pair in enumerate(PAIRS)}

    one = jnp.ones((1, LANES), jnp.float32)
    res, direction, pres = [one], [one], [None] * ITERS
    norm = gram[(0, 0)]
    for iteration in range(ITERS):
        applied = [None] + direction
        step_len = norm / combine(direction, applied, gram)
        for i, x in enumerate(direction):
            pres[i] = step_len * x if pres[i] is None else pres[i] + step_len * x
        new_res = []
        for i, x in enumerate(applied):
            old = res[i] if i < len(res) else None
            if x is None:
                new_res.append(old)
            elif old is None:
                new_res.append(-(step_len * x))
            else:
                new_res.append(old - step_len * x)
        res = new_res
        if iteration + 1 < ITERS:
            norm_next = combine(res, res, gram)
            ratio = norm_next / norm
            direction = [
                x + ratio * direction[i] if i < len(direction) else x for i, x in enumerate(res)
            ]
            norm = norm_next

    pres = [jnp.broadcast_to(x[:, 0:1], (POLY, extent2)) for x in pres]
    res = [jnp.broadcast_to(x[:, 0:1], (POLY, extent2)) for x in res]

    def finish(step, carry):
        at = pl.ds(pl.multiple_of(step * POLY, POLY), POLY)
        vec = [basis[i, at, :] for i in range(ITERS + 1)]
        out = pres[0] * vec[0]
        for i in range(1, ITERS):
            out = out + pres[i] * vec[i]
        pressure[at, :] = out
        out = res[0] * vec[0]
        for i in range(1, ITERS + 1):
            out = out + res[i] * vec[i]
        residual[at, :] = out
        return carry

    lax.fori_loop(0, rows // POLY, finish, 0)

    for peer in span_peers:
        points_copy(peer, me_p).wait_send()
        sum1_copy(peer, me_p).wait_send()
    for peer in stream_peers:
        sum2_copy(peer, me_s).wait_send()
    for k in range(ITERS + 1):
        for d in range(len(OFFSETS)):

            @pl.when(exists(OFFSETS[d]))
            def _(k=k, d=d):
                halo_copy(k, d).wait_send()


def on_device(velocity, coefficient, coords, forces, line_id, line_gain, dest_span, owner_element):
    extent0, extent1, extent2 = coefficient.shape
    rows = extent0 * extent1
    points = coords.shape[1]
    n_stream, n_span = lax.axis_size("stream"), lax.axis_size("span")
    capacity = max(2, 2 * points // n_span)
    total_pts = n_span * capacity
    tables = constants(extent0, extent1)
    f32 = jnp.float32
    block = jax.ShapeDtypeStruct((rows, extent2), f32)
    vmem = pl.BlockSpec(memory_space=pltpu.VMEM)
    hbm = pl.BlockSpec(memory_space=pl.ANY)
    steps = ITERS + 1
    sizes = (n_stream, n_span, extent0, extent1, extent2, capacity)
    pressure, residual = pl.pallas_call(
        functools.partial(body, sizes),
        out_shape=(block, block),
        in_specs=[hbm, hbm] + [vmem] * 12,
        out_specs=(vmem, vmem),
        scratch_shapes=[
            pltpu.VMEM((3, rows, extent2), f32),
            pltpu.VMEM((rows, extent2), f32),
            pltpu.VMEM((steps, rows, extent2), f32),
            pltpu.VMEM((rows, extent2), f32),
            pltpu.VMEM((rows, extent2), f32),
            pltpu.VMEM((n_span, 8, LANES), f32),
            pltpu.VMEM((n_span, 8, LANES), f32),
            pltpu.VMEM((3 * rows, total_pts), f32),
            pltpu.VMEM((extent2, total_pts), f32),
            pltpu.VMEM((steps, 2, extent1, extent2), f32),
            pltpu.VMEM((steps, 2, extent1, extent2), f32),
            pltpu.VMEM((steps, 2, extent0, extent2), f32),
            pltpu.VMEM((steps, 2, extent0, extent2), f32),
            pltpu.VMEM((steps, 4, 1, extent2), f32),
            pltpu.VMEM((steps, 4, 1, extent2), f32),
            pltpu.VMEM((n_span, 16, LANES), f32),
            pltpu.VMEM((n_stream, 16, LANES), f32),
            pltpu.SemaphoreType.DMA((4,)),
            pltpu.SemaphoreType.DMA((n_span,)),
            pltpu.SemaphoreType.DMA((n_span,)),
            pltpu.SemaphoreType.DMA((steps, 8)),
            pltpu.SemaphoreType.DMA((steps, 8)),
            pltpu.SemaphoreType.DMA((n_span,)),
            pltpu.SemaphoreType.DMA((n_span,)),
            pltpu.SemaphoreType.DMA((n_stream,)),
            pltpu.SemaphoreType.DMA((n_stream,)),
        ],
        compiler_params=pltpu.CompilerParams(
            collective_id=0, has_side_effects=True, vmem_limit_bytes=32 * 1024 * 1024
        ),
        cost_estimate=pl.CostEstimate(
            flops=6 * 10**9, bytes_accessed=4 * 2**20, transcendentals=10**4
        ),
        name="wind_farm_step",
    )(
        velocity.reshape(3, rows, extent2),
        coefficient.reshape(rows, extent2),
        coords,
        forces,
        line_id.reshape(1, points),
        line_gain.reshape(1, -1),
        dest_span.reshape(1, points),
        owner_element.reshape(1, points),
        *[jnp.asarray(table) for table in tables],
    )
    shape = (extent0, extent1, extent2)
    return pressure.reshape(shape), residual.reshape(shape)


def solution(mesh):
    return jax.shard_map(
        on_device,
        mesh=mesh,
        in_specs=(
            P(None, "stream", "span", None),
            P("stream", "span", None),
            P(None, ("stream", "span")),
            P(None, ("stream", "span")),
            P(("stream", "span")),
            P(),
            P(("stream", "span"), None),
            P(("stream", "span")),
        ),
        out_specs=(P("stream", "span", None), P("stream", "span", None)),
        check_vma=False,
    )
```

```python
import functools

import jax
import jax.numpy as jnp
import numpy as np
from jax import lax
from jax.experimental import pallas as pl
from jax.experimental.pallas import tpu as pltpu
from jax.sharding import PartitionSpec as P

POLY = 8
ITERS = 3
LANES = 128
CHUNK = 256
PARTS = 2
N_IN = 14

kernel_width = 0.45
gll_nodes = [
    -1.0,
    -0.8717401485096066,
    -0.5917001814331423,
    -0.2092992179024789,
    0.2092992179024789,
    0.5917001814331423,
    0.8717401485096066,
    1.0,
]
MESH = pl.DeviceIdType.MESH
OFFSETS = [(1, 0), (-1, 0), (0, 1), (0, -1), (1, 1), (1, -1), (-1, 1), (-1, -1)]


def legendre_value(point, degree):
    previous = 1.0
    current = point
    for order in range(1, degree):
        following = ((2 * order + 1) * point * current - order * previous) / (order + 1)
        previous = current
        current = following
    return current


def gll_tables():
    degree = POLY - 1
    values = [legendre_value(point, degree) for point in gll_nodes]
    weights = [2.0 / (degree * (degree + 1) * value * value) for value in values]
    diffmat = np.zeros((POLY, POLY))
    for i in range(POLY):
        for j in range(POLY):
            if i != j:
                diffmat[i, j] = values[i] / (values[j] * (gll_nodes[i] - gll_nodes[j]))
    diffmat[0, 0] = -degree * (degree + 1) / 4.0
    diffmat[-1, -1] = degree * (degree + 1) / 4.0
    return (
        np.asarray(gll_nodes, np.float32),
        np.asarray(weights, np.float32),
        np.asarray(diffmat, np.float32),
    )


def constants(extent0, extent1):
    nodes, weights, diffmat = gll_tables()
    eye = functools.partial(np.eye, dtype=np.float32)
    along0 = np.kron(eye(extent0 // POLY), np.kron(diffmat, eye(extent1)))
    along1 = np.kron(eye(extent0 * extent1 // POLY), diffmat)
    rows = np.concatenate([along0, along1], axis=0)
    cols = np.kron(eye(CHUNK // POLY), diffmat)

    row_weight = np.kron(np.tile(weights, extent0 // POLY), np.tile(weights, extent1 // POLY))
    row_weight = row_weight.astype(np.float32)
    weight = row_weight[:, None] * np.tile(weights, CHUNK // POLY)[None, :]
    column = np.repeat(nodes[:, None], LANES, axis=1)
    return rows, rows.T.copy(), cols.T.copy(), cols, weight, column


def split2(value):
    high = value.astype(jnp.bfloat16)
    low = (value - high.astype(jnp.float32)).astype(jnp.bfloat16)
    return high, low


def split3(value):
    high = value.astype(jnp.bfloat16)
    rest = value - high.astype(jnp.float32)
    middle = rest.astype(jnp.bfloat16)
    low = (rest - middle.astype(jnp.float32)).astype(jnp.bfloat16)
    return high, middle, low


def dot(first, second):
    return jnp.dot(first, second, preferred_element_type=jnp.float32)


def dot_nt(first, second):
    return lax.dot_general(
        first, second, (((1,), (1,)), ((), ())), preferred_element_type=jnp.float32
    )


def stacked(value, axis):
    high, low = split2(value)
    return jnp.concatenate([high, low, high], axis=axis)


def combine(first, second, moments, shift):
    total = 0.0
    for i, x in enumerate(first):
        for j, y in enumerate(second):
            total = total + x * y * moments[i + j + shift]
    return total


def body(sizes, *refs):
    n_stream, n_span, extent0, extent1, extent2, capacity = sizes
    hbm_in, (pressure, residual) = refs[:N_IN], refs[N_IN : N_IN + 2]
    vmem_in = refs[N_IN + 2 : 2 * N_IN + 2]
    (
        rows_fwd,
        rows_bwd,
        cols_fwd,
        cols_bwd,
        basis,
        work,
        joined,
        out_pts,
        in_pts,
        lhs_pts,
        rhs_pts,
        recv_stream,
        send_span,
        recv_span,
        send_edge,
        recv_edge,
        sums1,
        sums2,
        load_sem,
        pts_send,
        pts_recv,
        halo_send,
        halo_recv,
        sum1_send,
        sum1_recv,
        sum2_send,
        sum2_recv,
    ) = refs[2 * N_IN + 2 :]
    (
        coords,
        forces,
        line_id,
        line_gain,
        dest_span,
        owner,
        nodes,
        rows_fwd_f32,
        rows_bwd_f32,
        cols_fwd_f32,
        cols_bwd_f32,
        weight,
        vel,
        metric,
    ) = vmem_in
    rows = extent0 * extent1
    me_s, me_p = lax.axis_index("stream"), lax.axis_index("span")

    def exists(offset):
        s, p = me_s + offset[0], me_p + offset[1]
        return (s >= 0) & (s < n_stream) & (p >= 0) & (p < n_span)

    def at_offset(offset):
        return (
            lax.rem(me_s + offset[0] + n_stream, n_stream),
            lax.rem(me_p + offset[1] + n_span, n_span),
        )

    span_peers = [lax.rem(me_p + j, n_span) for j in range(1, n_span)]
    stream_peers = [lax.rem(me_s + j, n_stream) for j in range(1, n_stream)]

    barrier = pltpu.get_barrier_semaphore()
    for peer in span_peers:
        pl.semaphore_signal(barrier, inc=1, device_id=(me_s, peer), device_id_type=MESH)
    for peer in stream_peers:
        pl.semaphore_signal(barrier, inc=1, device_id=(peer, me_p), device_id_type=MESH)
    greeted = n_span - 1 + n_stream - 1
    for offset in OFFSETS[4:]:

        @pl.when(exists(offset))
        def _(offset=offset):
            pl.semaphore_signal(
                barrier, inc=1, device_id=at_offset(offset), device_id_type=MESH
            )

        greeted = greeted + exists(offset).astype(jnp.int32)

    loads = [
        pltpu.make_async_copy(hbm_in[n], vmem_in[n], load_sem.at[n]) for n in range(N_IN)
    ]
    for load in loads:
        load.start()

    def from_offset(d):
        return exists((-OFFSETS[d][0], -OFFSETS[d][1]))

    for d in range(8):
        buffer = (recv_stream, recv_span, recv_edge)[0 if d < 2 else 1 if d < 4 else 2]
        at = d if d < 2 else d - 2 if d < 4 else d - 4

        @pl.when(jnp.logical_not(from_offset(d)))
        def _(buffer=buffer, at=at):
            for k in range(ITERS + 1):
                buffer[k, at] = jnp.zeros(buffer.shape[2:], jnp.float32)

    points = coords.shape[1]
    group = LANES // capacity
    groups = n_span // group
    lines = line_gain.shape[1]
    earlier = (
        lax.broadcasted_iota(jnp.int32, (points, points), 0)
        < lax.broadcasted_iota(jnp.int32, (points, points), 1)
    ).astype(jnp.bfloat16)
    for load in loads[:7]:
        load.wait()
    ids = line_id[...]
    chosen = (lax.broadcasted_iota(jnp.int32, (lines, points), 0) == ids).astype(jnp.bfloat16)
    gain = sum(dot(part, chosen) for part in reversed(split3(line_gain[...])))
    scaled = forces[...] * gain
    target = dest_span[...]
    spans_at = lax.broadcasted_iota(jnp.int32, (n_span, points), 0)
    named = (spans_at == target).astype(jnp.float32)
    before = dot(named.astype(jnp.bfloat16), earlier)
    rank = jnp.sum(named * before, axis=0, keepdims=True).astype(jnp.int32)
    slot = target * LANES + lax.rem(me_p, group) * capacity + rank
    payload = jnp.concatenate(
        [
            coords[...],
            scaled,
            owner[...].astype(jnp.float32),
            jnp.zeros((1, points), jnp.float32),
        ],
        axis=0,
    )
    parts = jnp.concatenate(
        [p.astype(jnp.float32) for p in split3(payload)], axis=0
    ).astype(jnp.bfloat16)
    for dest in range(n_span):
        placed = (
            lax.broadcasted_iota(jnp.int32, (LANES, points), 0) + dest * LANES == slot
        ).astype(jnp.float32).astype(jnp.bfloat16)
        tile = dot_nt(parts, placed)
        out_pts[dest] = (tile[16:24] + tile[8:16]) + tile[0:8]

    for load in loads[7:12]:
        load.wait()
    high, low = split2(rows_fwd_f32[...])
    rows_fwd[...] = jnp.concatenate([high, high, low, low], axis=1)
    high, low = split2(rows_bwd_f32[...])
    rows_bwd[...] = jnp.concatenate([high, high, low], axis=1)
    for matrix, out in ((cols_fwd_f32, cols_fwd), (cols_bwd_f32, cols_bwd)):
        high, low = split2(matrix[...])
        out[...] = jnp.concatenate([high, high, low], axis=0)

    pl.semaphore_wait(barrier, greeted)

    def points_copy(peer, slot_at):
        return pltpu.make_async_remote_copy(
            src_ref=out_pts.at[peer],
            dst_ref=in_pts.at[slot_at],
            send_sem=pts_send.at[peer],
            recv_sem=pts_recv.at[slot_at],
            device_id=(me_s, peer),
            device_id_type=MESH,
        )

    for peer in span_peers:
        points_copy(peer, me_p).start()
    in_pts[me_p] = out_pts[me_p]

    chunks = [slice(c, c + CHUNK) for c in range(0, extent2, CHUNK)]
    for load in loads[12:]:
        load.wait()
    for cols in chunks:
        metric[:, cols] = metric[:, cols] * weight[...]

    for peer in span_peers:
        points_copy(peer, peer).wait_recv()

    elems2 = extent2 // POLY
    node_col = nodes[...]
    for g in range(groups):
        tile = in_pts[g * group]
        for i in range(1, group):
            tile = tile + in_pts[g * group + i]
        lanes = slice(g * LANES, (g + 1) * LANES)
        kern = [
            jnp.exp(-(((node_col - tile[k : k + 1]) / kernel_width) ** 2)) for k in range(3)
        ]
        elem = tile[6:7].astype(jnp.int32)
        elem_y = lax.rem(lax.div(elem, elems2), extent1 // POLY)
        elem_x = lax.div(elem, elems2 * (extent1 // POLY))
        elem_z = lax.rem(elem, elems2)
        for c in range(3):
            for a in range(extent0):
                for ey in range(extent1 // POLY):
                    mine = (elem_x == a // POLY) & (elem_y == ey)
                    factor = tile[3 + c : 4 + c] * kern[0][a % POLY : a % POLY + 1]
                    base = c * rows + a * extent1 + ey * POLY
                    lhs_pts[base : base + POLY, lanes] = jnp.where(mine, factor, 0.0) * kern[1]
        for ez in range(elems2):
            rhs_pts[ez * POLY : (ez + 1) * POLY, lanes] = jnp.where(elem_z == ez, kern[2], 0.0)

    left_pts = stacked(lhs_pts[...], 1)

    def tile_sum(value):
        total = jnp.sum(value.reshape(rows // POLY, POLY, CHUNK), axis=0)
        return sum(total[:, at : at + LANES] for at in range(0, CHUNK, LANES))

    def rhs_chunk(cols):
        high, low = split2(rhs_pts[cols, :])
        force = dot_nt(left_pts, jnp.concatenate([high, high, low], axis=1))
        part = [
            weight[...] * (vel[c, :, cols] + force[c * rows : (c + 1) * rows]) for c in range(3)
        ]
        both = jnp.concatenate(part[:2], axis=0)
        work[0, :, cols] = dot(rows_bwd[...], stacked(both, 0)) + dot(
            stacked(part[2], 1), cols_bwd[...]
        )

    def operator_chunk(k, cols):
        field = basis[k, :, cols]
        high, low = split2(field)
        m = metric[:, cols]
        grad = dot(rows_fwd[...], jnp.concatenate([high, low, high, low], axis=0))
        grad2 = dot(jnp.concatenate([high, low, high], axis=1), cols_fwd[...])
        both = jnp.concatenate([grad[:rows] * m, grad[rows:] * m], axis=0)
        out = (
            dot(rows_bwd[...], stacked(both, 0))
            + dot(stacked(grad2 * m, 1), cols_bwd[...])
            + weight[...] * field
        )
        work[k + 1, :, cols] = out
        return tile_sum(field * work[k, :, cols]), tile_sum(field * out)

    last0, last1 = extent0 - 1, extent1 - 1
    part_width = extent2 // PARTS

    def halo_copy(k, d, q):
        cols = pl.ds(q * part_width, part_width)
        if d < 2:
            src = work.at[k, pl.ds(last0 * extent1 if d == 0 else 0, extent1), cols]
            dst = recv_stream.at[k, d, :, cols]
        elif d < 4:
            src, dst = send_span.at[k, d - 2, :, cols], recv_span.at[k, d - 2, :, cols]
        else:
            src, dst = send_edge.at[k, d - 4, :, cols], recv_edge.at[k, d - 4, :, cols]
        return pltpu.make_async_remote_copy(
            src_ref=src,
            dst_ref=dst,
            send_sem=halo_send.at[k, d, q],
            recv_sem=halo_recv.at[k, d, q],
            device_id=at_offset(OFFSETS[d]),
            device_id_type=MESH,
        )

    def send_faces(k, q):
        cols = slice(q * part_width, (q + 1) * part_width)
        for a in range(extent0):
            top = work[k, a * extent1 + last1 : a * extent1 + last1 + 1, cols]
            bottom = work[k, a * extent1 : a * extent1 + 1, cols]
            send_span[k, 0, a : a + 1, cols] = top
            send_span[k, 1, a : a + 1, cols] = bottom
            if a == last0:
                send_edge[k, 0, :, cols] = top
                send_edge[k, 1, :, cols] = bottom
            if a == 0:
                send_edge[k, 2, :, cols] = top
                send_edge[k, 3, :, cols] = bottom
        for d in range(8):

            @pl.when(exists(OFFSETS[d]))
            def _(d=d):
                halo_copy(k, d, q).start()

    def join(k, q):
        for d in (2, 3, 4, 5, 6, 7, 0, 1):

            @pl.when(from_offset(d))
            def _(d=d):
                halo_copy(k, d, q).wait_recv()

        cols = slice(q * part_width, (q + 1) * part_width)
        sub = lax.broadcasted_iota(jnp.int32, (POLY, part_width), 0)
        for a in range(extent0):
            tiles = []
            for ey in range(extent1 // POLY):
                base = a * extent1 + ey * POLY
                x = work[k, base : base + POLY, cols]
                if a == 0:
                    x = x + recv_stream[k, 0, ey * POLY : (ey + 1) * POLY, cols]
                if a == last0:
                    x = x + recv_stream[k, 1, ey * POLY : (ey + 1) * POLY, cols]
                tiles.append(x)
            lower = recv_span[k, 0, a : a + 1, cols]
            upper = recv_span[k, 1, a : a + 1, cols]
            if a == 0:
                lower = lower + recv_edge[k, 0, :, cols]
                upper = upper + recv_edge[k, 1, :, cols]
            if a == last0:
                lower = lower + recv_edge[k, 2, :, cols]
                upper = upper + recv_edge[k, 3, :, cols]
            for ey, x in enumerate(tiles):
                below = lower if ey == 0 else pltpu.roll(tiles[ey - 1], 1, 0)
                above = upper if ey + 1 == len(tiles) else pltpu.roll(tiles[ey + 1], POLY - 1, 0)
                base = a * extent1 + ey * POLY
                joined[base : base + POLY, cols] = (
                    x + jnp.where(sub == 0, below, 0.0) + jnp.where(sub == POLY - 1, above, 0.0)
                )

    def assemble(k, cols):
        start, stop = max(cols.start - LANES, 0), min(cols.stop + LANES, extent2)
        width = stop - start
        lane = lax.broadcasted_iota(jnp.int32, (POLY, CHUNK), 1) + cols.start
        first2 = (lane % POLY == 0) & (lane > 0)
        last2 = (lane % POLY == POLY - 1) & (lane < extent2 - 1)
        inner = slice(cols.start - start, cols.stop - start)
        for base in range(0, rows, POLY):
            x = joined[base : base + POLY, start:stop]
            lower = pltpu.roll(x, 1, 1)[:, inner]
            upper = pltpu.roll(x, width - 1, 1)[:, inner]
            basis[k, base : base + POLY, cols] = (
                x[:, inner] + jnp.where(first2, lower, 0.0) + jnp.where(last2, upper, 0.0)
            )

    per_part = len(chunks) // PARTS

    def joined_chunks(k):
        have = 0
        for n, cols in enumerate(chunks):
            need = min((n + 1) // per_part + 1, PARTS)
            while have < need:
                join(k, have)
                have += 1
            assemble(k, cols)
            yield n, cols

    for n, cols in enumerate(chunks):
        rhs_chunk(cols)
        if (n + 1) % per_part == 0:
            send_faces(0, n // per_part)
    mine = []
    for k in range(ITERS):
        even = odd = 0.0
        for n, cols in joined_chunks(k):
            more = operator_chunk(k, cols)
            even, odd = even + more[0], odd + more[1]
            if (n + 1) % per_part == 0:
                send_faces(k + 1, n // per_part)
        mine += [even, odd]

    mine = [jnp.sum(total, axis=0, keepdims=True) for total in mine]
    mine.append(jnp.zeros((8 - len(mine), LANES), jnp.float32))
    sums1[me_p] = jnp.concatenate(mine, axis=0)

    def sum1_copy(peer, slot_at):
        return pltpu.make_async_remote_copy(
            src_ref=sums1.at[me_p],
            dst_ref=sums1.at[slot_at],
            send_sem=sum1_send.at[peer],
            recv_sem=sum1_recv.at[slot_at],
            device_id=(me_s, peer),
            device_id_type=MESH,
        )

    def sum2_copy(peer, slot_at):
        return pltpu.make_async_remote_copy(
            src_ref=sums2.at[me_s],
            dst_ref=sums2.at[slot_at],
            send_sem=sum2_send.at[peer],
            recv_sem=sum2_recv.at[slot_at],
            device_id=(peer, me_p),
            device_id_type=MESH,
        )

    for peer in span_peers:
        sum1_copy(peer, me_p).start()
    for peer in span_peers:
        sum1_copy(peer, peer).wait_recv()
    total = sums1[0]
    for i in range(1, n_span):
        total = total + sums1[i]
    sums2[me_s] = total
    for peer in stream_peers:
        sum2_copy(peer, me_s).start()
    for _ in joined_chunks(ITERS):
        pass
    for peer in stream_peers:
        sum2_copy(peer, peer).wait_recv()
    total = sums2[0]
    for i in range(1, n_stream):
        total = total + sums2[i]
    total = jnp.broadcast_to(jnp.sum(total, axis=1, keepdims=True), (8, LANES))
    moments = [total[n : n + 1] for n in range(2 * ITERS)]

    one = jnp.ones((1, LANES), jnp.float32)
    res, direction, pres = [one], [one], [0.0] * ITERS
    norm = moments[0]
    for iteration in range(ITERS):
        step_len = norm / combine(direction, direction, moments, 1)
        for i, x in enumerate(direction):
            pres[i] = pres[i] + step_len * x
        res = res + [0.0]
        res = [res[0]] + [x - step_len * y for x, y in zip(res[1:], direction)]
        if iteration + 1 < ITERS:
            norm_next = combine(res, res, moments, 0)
            ratio = norm_next / norm
            direction = [x + ratio * y for x, y in zip(res, direction + [0.0])]
            norm = norm_next

    pres = [jnp.broadcast_to(x[:, 0:1], (POLY, extent2)) for x in pres]
    res = [jnp.broadcast_to(x[:, 0:1], (POLY, extent2)) for x in res]

    def finish(step, carry):
        at = pl.ds(pl.multiple_of(step * POLY, POLY), POLY)
        vec = [basis[i, at, :] for i in range(ITERS + 1)]
        out = pres[0] * vec[0]
        for i in range(1, ITERS):
            out = out + pres[i] * vec[i]
        pressure[at, :] = out
        out = res[0] * vec[0]
        for i in range(1, ITERS + 1):
            out = out + res[i] * vec[i]
        residual[at, :] = out
        return carry

    lax.fori_loop(0, rows // POLY, finish, 0)

    for peer in span_peers:
        points_copy(peer, me_p).wait_send()
        sum1_copy(peer, me_p).wait_send()
    for peer in stream_peers:
        sum2_copy(peer, me_s).wait_send()
    for d in range(8):

        @pl.when(exists(OFFSETS[d]))
        def _(d=d):
            for k in range(ITERS + 1):
                for q in range(PARTS):
                    halo_copy(k, d, q).wait_send()


def on_device(velocity, coefficient, coords, forces, line_id, line_gain, dest_span, owner_element):
    extent0, extent1, extent2 = coefficient.shape
    rows = extent0 * extent1
    points = coords.shape[1]
    n_stream, n_span = lax.axis_size("stream"), lax.axis_size("span")
    capacity = max(2, 2 * points // n_span)
    total_pts = n_span * capacity
    tables = constants(extent0, extent1)
    f32 = jnp.float32
    block = jax.ShapeDtypeStruct((rows, extent2), f32)
    vmem = pl.BlockSpec(memory_space=pltpu.VMEM)
    hbm = pl.BlockSpec(memory_space=pl.ANY)
    steps = ITERS + 1
    sizes = (n_stream, n_span, extent0, extent1, extent2, capacity)
    rows_fwd, rows_bwd, cols_fwd, cols_bwd, weight, column = [jnp.asarray(x) for x in tables]
    operands = [
        coords,
        forces,
        line_id.reshape(1, points),
        line_gain.reshape(1, -1),
        dest_span.reshape(1, points),
        owner_element.reshape(1, points),
        column,
        rows_fwd,
        rows_bwd,
        cols_fwd,
        cols_bwd,
        weight,
        velocity.reshape(3, rows, extent2),
        coefficient.reshape(rows, extent2),
    ]
    pressure, residual = pl.pallas_call(
        functools.partial(body, sizes),
        out_shape=(block, block),
        in_specs=[hbm] * N_IN,
        out_specs=(vmem, vmem),
        scratch_shapes=[pltpu.VMEM(x.shape, x.dtype) for x in operands]
        + [
            pltpu.VMEM((2 * rows, 4 * rows), jnp.bfloat16),
            pltpu.VMEM((rows, 6 * rows), jnp.bfloat16),
            pltpu.VMEM((3 * CHUNK, CHUNK), jnp.bfloat16),
            pltpu.VMEM((3 * CHUNK, CHUNK), jnp.bfloat16),
            pltpu.VMEM((steps, rows, extent2), f32),
            pltpu.VMEM((steps, rows, extent2), f32),
            pltpu.VMEM((rows, extent2), f32),
            pltpu.VMEM((n_span, 8, LANES), f32),
            pltpu.VMEM((n_span, 8, LANES), f32),
            pltpu.VMEM((3 * rows, total_pts), f32),
            pltpu.VMEM((extent2, total_pts), f32),
            pltpu.VMEM((steps, 2, extent1, extent2), f32),
            pltpu.VMEM((steps, 2, extent0, extent2), f32),
            pltpu.VMEM((steps, 2, extent0, extent2), f32),
            pltpu.VMEM((steps, 4, 1, extent2), f32),
            pltpu.VMEM((steps, 4, 1, extent2), f32),
            pltpu.VMEM((n_span, 8, LANES), f32),
            pltpu.VMEM((n_stream, 8, LANES), f32),
            pltpu.SemaphoreType.DMA((N_IN,)),
            pltpu.SemaphoreType.DMA((n_span,)),
            pltpu.SemaphoreType.DMA((n_span,)),
            pltpu.SemaphoreType.DMA((steps, 8, PARTS)),
            pltpu.SemaphoreType.DMA((steps, 8, PARTS)),
            pltpu.SemaphoreType.DMA((n_span,)),
            pltpu.SemaphoreType.DMA((n_span,)),
            pltpu.SemaphoreType.DMA((n_stream,)),
            pltpu.SemaphoreType.DMA((n_stream,)),
        ],
        compiler_params=pltpu.CompilerParams(
            collective_id=0, has_side_effects=True, vmem_limit_bytes=60 * 1024 * 1024
        ),
        cost_estimate=pl.CostEstimate(
            flops=6 * 10**9, bytes_accessed=4 * 2**20, transcendentals=10**4
        ),
        name="wind_farm_step",
    )(*operands)
    shape = (extent0, extent1, extent2)
    return pressure.reshape(shape), residual.reshape(shape)


def solution(mesh):
    return jax.shard_map(
        on_device,
        mesh=mesh,
        in_specs=(
            P(None, "stream", "span", None),
            P("stream", "span", None),
            P(None, ("stream", "span")),
            P(None, ("stream", "span")),
            P(("stream", "span")),
            P(),
            P(("stream", "span"), None),
            P(("stream", "span")),
        ),
        out_specs=(P("stream", "span", None), P("stream", "span", None)),
        check_vma=False,
    )
```

```python
import functools

import jax
import jax.numpy as jnp
import numpy as np
from jax import lax
from jax.experimental import pallas as pl
from jax.experimental.pallas import tpu as pltpu
from jax.sharding import PartitionSpec as P

POLY = 8
ITERS = 3
LANES = 128
CHUNK = 256
PARTS = 2
N_IN = 14

kernel_width = 0.45
gll_nodes = [
    -1.0,
    -0.8717401485096066,
    -0.5917001814331423,
    -0.2092992179024789,
    0.2092992179024789,
    0.5917001814331423,
    0.8717401485096066,
    1.0,
]
MESH = pl.DeviceIdType.MESH
OFFSETS = [(1, 0), (-1, 0), (0, 1), (0, -1), (1, 1), (1, -1), (-1, 1), (-1, -1)]


def legendre_value(point, degree):
    previous = 1.0
    current = point
    for order in range(1, degree):
        following = ((2 * order + 1) * point * current - order * previous) / (order + 1)
        previous = current
        current = following
    return current


def gll_tables():
    degree = POLY - 1
    values = [legendre_value(point, degree) for point in gll_nodes]
    weights = [2.0 / (degree * (degree + 1) * value * value) for value in values]
    diffmat = np.zeros((POLY, POLY))
    for i in range(POLY):
        for j in range(POLY):
            if i != j:
                diffmat[i, j] = values[i] / (values[j] * (gll_nodes[i] - gll_nodes[j]))
    diffmat[0, 0] = -degree * (degree + 1) / 4.0
    diffmat[-1, -1] = degree * (degree + 1) / 4.0
    return (
        np.asarray(gll_nodes, np.float32),
        np.asarray(weights, np.float32),
        np.asarray(diffmat, np.float32),
    )


def constants(extent0, extent1):
    nodes, weights, diffmat = gll_tables()
    eye = functools.partial(np.eye, dtype=np.float32)
    along0 = np.kron(eye(extent0 // POLY), np.kron(diffmat, eye(extent1)))
    along1 = np.kron(eye(extent0 * extent1 // POLY), diffmat)
    rows = np.concatenate([along0, along1], axis=0)
    cols = np.kron(eye(CHUNK // POLY), diffmat)

    row_weight = np.kron(np.tile(weights, extent0 // POLY), np.tile(weights, extent1 // POLY))
    row_weight = row_weight.astype(np.float32)
    weight = row_weight[:, None] * np.tile(weights, CHUNK // POLY)[None, :]
    table = np.concatenate([nodes[:, None], weights[:, None], diffmat.T * weights[None, :]], axis=1)
    column = np.repeat(table.T.reshape(-1, 1), LANES, axis=1)
    return rows, rows.T.copy(), cols.T.copy(), cols, weight, column


def split2(value):
    high = value.astype(jnp.bfloat16)
    low = (value - high.astype(jnp.float32)).astype(jnp.bfloat16)
    return high, low


def split3(value):
    high = value.astype(jnp.bfloat16)
    rest = value - high.astype(jnp.float32)
    middle = rest.astype(jnp.bfloat16)
    low = (rest - middle.astype(jnp.float32)).astype(jnp.bfloat16)
    return high, middle, low


def dot(first, second):
    return jnp.dot(first, second, preferred_element_type=jnp.float32)


def dot_nt(first, second):
    return lax.dot_general(
        first, second, (((1,), (1,)), ((), ())), preferred_element_type=jnp.float32
    )


def stacked(value, axis):
    high, low = split2(value)
    return jnp.concatenate([high, low, high], axis=axis)


def combine(first, second, moments, shift):
    total = 0.0
    for i, x in enumerate(first):
        for j, y in enumerate(second):
            total = total + x * y * moments[i + j + shift]
    return total


def body(sizes, *refs):
    n_stream, n_span, extent0, extent1, extent2, capacity = sizes
    n_out = 3 * ITERS + 2
    hbm_in, outs = refs[:N_IN], refs[N_IN : N_IN + n_out]
    basis_out, factors = outs[: ITERS + 1], outs[ITERS + 1 :]
    vmem_in = refs[N_IN + n_out : 2 * N_IN + n_out]
    (
        rows_fwd,
        rows_bwd,
        cols_fwd,
        cols_bwd,
        basis,
        work,
        joined,
        out_pts,
        in_pts,
        lhs_pts,
        rhs_pts,
        recv_stream,
        send_span,
        recv_span,
        send_edge,
        recv_edge,
        sums1,
        sums2,
        load_sem,
        store_sem,
        pts_send,
        pts_recv,
        halo_send,
        halo_recv,
        sum1_send,
        sum1_recv,
        sum2_send,
        sum2_recv,
    ) = refs[2 * N_IN + n_out :]
    (
        coords,
        forces,
        line_id,
        line_gain,
        dest_span,
        owner,
        nodes,
        rows_fwd_f32,
        rows_bwd_f32,
        cols_fwd_f32,
        cols_bwd_f32,
        weight,
        vel,
        metric,
    ) = vmem_in
    rows = extent0 * extent1
    me_s, me_p = lax.axis_index("stream"), lax.axis_index("span")

    def exists(offset):
        s, p = me_s + offset[0], me_p + offset[1]
        return (s >= 0) & (s < n_stream) & (p >= 0) & (p < n_span)

    def at_offset(offset):
        return (
            lax.rem(me_s + offset[0] + n_stream, n_stream),
            lax.rem(me_p + offset[1] + n_span, n_span),
        )

    span_peers = [lax.rem(me_p + j, n_span) for j in range(1, n_span)]
    stream_peers = [lax.rem(me_s + j, n_stream) for j in range(1, n_stream)]

    barrier = pltpu.get_barrier_semaphore()
    for peer in span_peers:
        pl.semaphore_signal(barrier, inc=1, device_id=(me_s, peer), device_id_type=MESH)
    for peer in stream_peers:
        pl.semaphore_signal(barrier, inc=1, device_id=(peer, me_p), device_id_type=MESH)
    greeted = n_span - 1 + n_stream - 1
    for offset in OFFSETS[4:]:

        @pl.when(exists(offset))
        def _(offset=offset):
            pl.semaphore_signal(
                barrier, inc=1, device_id=at_offset(offset), device_id_type=MESH
            )

        greeted = greeted + exists(offset).astype(jnp.int32)

    loads = [
        pltpu.make_async_copy(hbm_in[n], vmem_in[n], load_sem.at[n]) for n in range(N_IN)
    ]
    for load in loads:
        load.start()

    def from_offset(d):
        return exists((-OFFSETS[d][0], -OFFSETS[d][1]))

    for d in range(8):
        buffer = (recv_stream, recv_span, recv_edge)[0 if d < 2 else 1 if d < 4 else 2]
        at = d if d < 2 else d - 2 if d < 4 else d - 4

        @pl.when(jnp.logical_not(from_offset(d)))
        def _(buffer=buffer, at=at):
            for k in range(ITERS + 1):
                buffer[k, at] = jnp.zeros(buffer.shape[2:], jnp.float32)

    points = coords.shape[1]
    group = LANES // capacity
    groups = n_span // group
    lines = line_gain.shape[1]
    earlier = (
        lax.broadcasted_iota(jnp.int32, (points, points), 0)
        < lax.broadcasted_iota(jnp.int32, (points, points), 1)
    ).astype(jnp.bfloat16)
    for load in loads[:7]:
        load.wait()
    ids = line_id[...]
    chosen = (lax.broadcasted_iota(jnp.int32, (lines, points), 0) == ids).astype(jnp.bfloat16)
    gain = sum(dot(part, chosen) for part in reversed(split3(line_gain[...])))
    scaled = forces[...] * gain
    target = dest_span[...]
    spans_at = lax.broadcasted_iota(jnp.int32, (n_span, points), 0)
    named = (spans_at == target).astype(jnp.float32)
    before = dot(named.astype(jnp.bfloat16), earlier)
    rank = jnp.sum(named * before, axis=0, keepdims=True).astype(jnp.int32)
    slot = target * LANES + lax.rem(me_p, group) * capacity + rank
    payload = jnp.concatenate(
        [
            coords[...],
            scaled,
            owner[...].astype(jnp.float32),
            jnp.zeros((1, points), jnp.float32),
        ],
        axis=0,
    )
    parts = jnp.concatenate(
        [p.astype(jnp.float32) for p in split3(payload)], axis=0
    ).astype(jnp.bfloat16)
    for dest in range(n_span):
        placed = (
            lax.broadcasted_iota(jnp.int32, (LANES, points), 0) + dest * LANES == slot
        ).astype(jnp.float32).astype(jnp.bfloat16)
        tile = dot_nt(parts, placed)
        out_pts[dest] = (tile[16:24] + tile[8:16]) + tile[0:8]

    for load in loads[7:12]:
        load.wait()
    high, low = split2(rows_fwd_f32[...])
    rows_fwd[...] = jnp.concatenate([high, high, low, low], axis=1)
    high, low = split2(rows_bwd_f32[...])
    rows_bwd[...] = jnp.concatenate([high, high, low], axis=1)
    for matrix, out in ((cols_fwd_f32, cols_fwd), (cols_bwd_f32, cols_bwd)):
        high, low = split2(matrix[...])
        out[...] = jnp.concatenate([high, high, low], axis=0)

    pl.semaphore_wait(barrier, greeted)

    def points_copy(peer, slot_at):
        return pltpu.make_async_remote_copy(
            src_ref=out_pts.at[peer],
            dst_ref=in_pts.at[slot_at],
            send_sem=pts_send.at[peer],
            recv_sem=pts_recv.at[slot_at],
            device_id=(me_s, peer),
            device_id_type=MESH,
        )

    for peer in span_peers:
        points_copy(peer, me_p).start()
    in_pts[me_p] = out_pts[me_p]

    chunks = [slice(c, c + CHUNK) for c in range(0, extent2, CHUNK)]
    for load in loads[12:]:
        load.wait()
    for cols in chunks:
        w = weight[...]
        both = jnp.concatenate([w * vel[0, :, cols], w * vel[1, :, cols]], axis=0)
        work[0, :, cols] = dot(rows_bwd[...], stacked(both, 0)) + dot(
            stacked(w * vel[2, :, cols], 1), cols_bwd[...]
        )
        metric[:, cols] = metric[:, cols] * w

    for peer in span_peers:
        points_copy(peer, peer).wait_recv()

    elems2 = extent2 // POLY
    total_pts = groups * LANES
    node_col = nodes[0:POLY]
    weight_col = nodes[POLY : 2 * POLY]
    diff_cols = [nodes[(2 + a) * POLY : (3 + a) * POLY] for a in range(POLY)]
    for g in range(groups):
        tile = in_pts[g * group]
        for i in range(1, group):
            tile = tile + in_pts[g * group + i]
        lanes = slice(g * LANES, (g + 1) * LANES)
        lanes_diff = slice(total_pts + g * LANES, total_pts + (g + 1) * LANES)
        plain, diff = [], []
        for k in range(3):
            kern = jnp.exp(-(((node_col - tile[k : k + 1]) / kernel_width) ** 2))
            plain.append(weight_col * kern)
            diff.append(sum(diff_cols[a] * kern[a : a + 1] for a in range(POLY)))
        elem = tile[6:7].astype(jnp.int32)
        elem_y = lax.rem(lax.div(elem, elems2), extent1 // POLY)
        elem_x = lax.div(elem, elems2 * (extent1 // POLY))
        elem_z = lax.rem(elem, elems2)
        for a in range(extent0):
            for ey in range(extent1 // POLY):
                mine = (elem_x == a // POLY) & (elem_y == ey)
                at = slice(a % POLY, a % POLY + 1)
                factor0 = jnp.where(mine, tile[3:4] * diff[0][at], 0.0)
                factor1 = jnp.where(mine, tile[4:5] * plain[0][at], 0.0)
                factor2 = jnp.where(mine, tile[5:6] * plain[0][at], 0.0)
                base = a * extent1 + ey * POLY
                lhs_pts[base : base + POLY, lanes] = factor0 * plain[1] + factor1 * diff[1]
                lhs_pts[base : base + POLY, lanes_diff] = factor2 * plain[1]
        for ez in range(elems2):
            at = slice(ez * POLY, (ez + 1) * POLY)
            rhs_pts[at, lanes] = jnp.where(elem_z == ez, plain[2], 0.0)
            rhs_pts[at, lanes_diff] = jnp.where(elem_z == ez, diff[2], 0.0)

    left_pts = stacked(lhs_pts[...], 1)

    def tile_sum(value):
        total = jnp.sum(value.reshape(rows // POLY, POLY, CHUNK), axis=0)
        return sum(total[:, at : at + LANES] for at in range(0, CHUNK, LANES))

    def rhs_chunk(cols):
        high, low = split2(rhs_pts[cols, :])
        force = dot_nt(left_pts, jnp.concatenate([high, high, low], axis=1))
        work[0, :, cols] = work[0, :, cols] + force

    def operator_chunk(k, cols):
        field = basis[k, :, cols]
        high, low = split2(field)
        m = metric[:, cols]
        grad = dot(rows_fwd[...], jnp.concatenate([high, low, high, low], axis=0))
        grad2 = dot(jnp.concatenate([high, low, high], axis=1), cols_fwd[...])
        both = jnp.concatenate([grad[:rows] * m, grad[rows:] * m], axis=0)
        out = (
            dot(rows_bwd[...], stacked(both, 0))
            + dot(stacked(grad2 * m, 1), cols_bwd[...])
            + weight[...] * field
        )
        work[k + 1, :, cols] = out
        return tile_sum(field * work[k, :, cols]), tile_sum(field * out)

    last0, last1 = extent0 - 1, extent1 - 1
    part_width = extent2 // PARTS

    def halo_copy(k, d, q):
        cols = pl.ds(q * part_width, part_width)
        if d < 2:
            src = work.at[k, pl.ds(last0 * extent1 if d == 0 else 0, extent1), cols]
            dst = recv_stream.at[k, d, :, cols]
        elif d < 4:
            src, dst = send_span.at[k, d - 2, :, cols], recv_span.at[k, d - 2, :, cols]
        else:
            src, dst = send_edge.at[k, d - 4, :, cols], recv_edge.at[k, d - 4, :, cols]
        return pltpu.make_async_remote_copy(
            src_ref=src,
            dst_ref=dst,
            send_sem=halo_send.at[k, d, q],
            recv_sem=halo_recv.at[k, d, q],
            device_id=at_offset(OFFSETS[d]),
            device_id_type=MESH,
        )

    def send_faces(k, q):
        cols = slice(q * part_width, (q + 1) * part_width)
        for a in range(extent0):
            top = work[k, a * extent1 + last1 : a * extent1 + last1 + 1, cols]
            bottom = work[k, a * extent1 : a * extent1 + 1, cols]
            send_span[k, 0, a : a + 1, cols] = top
            send_span[k, 1, a : a + 1, cols] = bottom
            if a == last0:
                send_edge[k, 0, :, cols] = top
                send_edge[k, 1, :, cols] = bottom
            if a == 0:
                send_edge[k, 2, :, cols] = top
                send_edge[k, 3, :, cols] = bottom
        for d in range(8):

            @pl.when(exists(OFFSETS[d]))
            def _(d=d):
                halo_copy(k, d, q).start()

    def join(k, q):
        for d in (2, 3, 4, 5, 6, 7, 0, 1):

            @pl.when(from_offset(d))
            def _(d=d):
                halo_copy(k, d, q).wait_recv()

        cols = slice(q * part_width, (q + 1) * part_width)
        sub = lax.broadcasted_iota(jnp.int32, (POLY, part_width), 0)
        for a in range(extent0):
            tiles = []
            for ey in range(extent1 // POLY):
                base = a * extent1 + ey * POLY
                x = work[k, base : base + POLY, cols]
                if a == 0:
                    x = x + recv_stream[k, 0, ey * POLY : (ey + 1) * POLY, cols]
                if a == last0:
                    x = x + recv_stream[k, 1, ey * POLY : (ey + 1) * POLY, cols]
                tiles.append(x)
            lower = recv_span[k, 0, a : a + 1, cols]
            upper = recv_span[k, 1, a : a + 1, cols]
            if a == 0:
                lower = lower + recv_edge[k, 0, :, cols]
                upper = upper + recv_edge[k, 1, :, cols]
            if a == last0:
                lower = lower + recv_edge[k, 2, :, cols]
                upper = upper + recv_edge[k, 3, :, cols]
            for ey, x in enumerate(tiles):
                below = lower if ey == 0 else pltpu.roll(tiles[ey - 1], 1, 0)
                above = upper if ey + 1 == len(tiles) else pltpu.roll(tiles[ey + 1], POLY - 1, 0)
                base = a * extent1 + ey * POLY
                joined[base : base + POLY, cols] = (
                    x + jnp.where(sub == 0, below, 0.0) + jnp.where(sub == POLY - 1, above, 0.0)
                )

    def assemble(k, cols):
        start, stop = max(cols.start - LANES, 0), min(cols.stop + LANES, extent2)
        width = stop - start
        lane = lax.broadcasted_iota(jnp.int32, (POLY, CHUNK), 1) + cols.start
        first2 = (lane % POLY == 0) & (lane > 0)
        last2 = (lane % POLY == POLY - 1) & (lane < extent2 - 1)
        inner = slice(cols.start - start, cols.stop - start)
        for base in range(0, rows, POLY):
            x = joined[base : base + POLY, start:stop]
            lower = pltpu.roll(x, 1, 1)[:, inner]
            upper = pltpu.roll(x, width - 1, 1)[:, inner]
            basis[k, base : base + POLY, cols] = (
                x[:, inner] + jnp.where(first2, lower, 0.0) + jnp.where(last2, upper, 0.0)
            )

    per_part = len(chunks) // PARTS

    def store(k):
        return pltpu.make_async_copy(basis.at[k], basis_out[k], store_sem.at[k])

    def joined_chunks(k):
        have = 0
        for n, cols in enumerate(chunks):
            need = min((n + 1) // per_part + 1, PARTS)
            while have < need:
                join(k, have)
                have += 1
            assemble(k, cols)
            if n + 1 == len(chunks):
                store(k).start()
            yield n, cols

    for n, cols in enumerate(chunks):
        rhs_chunk(cols)
        if (n + 1) % per_part == 0:
            send_faces(0, n // per_part)
    mine = []
    for k in range(ITERS):
        even = odd = 0.0
        for n, cols in joined_chunks(k):
            more = operator_chunk(k, cols)
            even, odd = even + more[0], odd + more[1]
            if (n + 1) % per_part == 0:
                send_faces(k + 1, n // per_part)
        mine += [even, odd]

    mine = [jnp.sum(total, axis=0, keepdims=True) for total in mine]
    mine.append(jnp.zeros((8 - len(mine), LANES), jnp.float32))
    sums1[me_p] = jnp.concatenate(mine, axis=0)

    def sum1_copy(peer, slot_at):
        return pltpu.make_async_remote_copy(
            src_ref=sums1.at[me_p],
            dst_ref=sums1.at[slot_at],
            send_sem=sum1_send.at[peer],
            recv_sem=sum1_recv.at[slot_at],
            device_id=(me_s, peer),
            device_id_type=MESH,
        )

    def sum2_copy(peer, slot_at):
        return pltpu.make_async_remote_copy(
            src_ref=sums2.at[me_s],
            dst_ref=sums2.at[slot_at],
            send_sem=sum2_send.at[peer],
            recv_sem=sum2_recv.at[slot_at],
            device_id=(peer, me_p),
            device_id_type=MESH,
        )

    for peer in span_peers:
        sum1_copy(peer, me_p).start()
    for peer in span_peers:
        sum1_copy(peer, peer).wait_recv()
    total = sums1[0]
    for i in range(1, n_span):
        total = total + sums1[i]
    sums2[me_s] = total
    for peer in stream_peers:
        sum2_copy(peer, me_s).start()
    for _ in joined_chunks(ITERS):
        pass
    for peer in stream_peers:
        sum2_copy(peer, peer).wait_recv()
    total = sums2[0]
    for i in range(1, n_stream):
        total = total + sums2[i]
    total = jnp.broadcast_to(jnp.sum(total, axis=1, keepdims=True), (8, LANES))
    moments = [total[n : n + 1] for n in range(2 * ITERS)]

    one = jnp.ones((1, LANES), jnp.float32)
    res, direction, pres = [one], [one], [0.0] * ITERS
    norm = moments[0]
    for iteration in range(ITERS):
        step_len = norm / combine(direction, direction, moments, 1)
        for i, x in enumerate(direction):
            pres[i] = pres[i] + step_len * x
        res = res + [0.0]
        res = [res[0]] + [x - step_len * y for x, y in zip(res[1:], direction)]
        if iteration + 1 < ITERS:
            norm_next = combine(res, res, moments, 0)
            ratio = norm_next / norm
            direction = [x + ratio * y for x, y in zip(res, direction + [0.0])]
            norm = norm_next

    for factor, value in zip(factors, pres + res):
        factor[...] = value[:, 0:1]

    for k in range(ITERS + 1):
        store(k).wait()
    for peer in span_peers:
        points_copy(peer, me_p).wait_send()
        sum1_copy(peer, me_p).wait_send()
    for peer in stream_peers:
        sum2_copy(peer, me_s).wait_send()
    for d in range(8):

        @pl.when(exists(OFFSETS[d]))
        def _(d=d):
            for k in range(ITERS + 1):
                for q in range(PARTS):
                    halo_copy(k, d, q).wait_send()


def on_device(velocity, coefficient, coords, forces, line_id, line_gain, dest_span, owner_element):
    extent0, extent1, extent2 = coefficient.shape
    rows = extent0 * extent1
    points = coords.shape[1]
    n_stream, n_span = lax.axis_size("stream"), lax.axis_size("span")
    capacity = max(2, 2 * points // n_span)
    total_pts = n_span * capacity
    tables = constants(extent0, extent1)
    f32 = jnp.float32
    block = jax.ShapeDtypeStruct((rows, extent2), f32)
    vmem = pl.BlockSpec(memory_space=pltpu.VMEM)
    hbm = pl.BlockSpec(memory_space=pl.ANY)
    steps = ITERS + 1
    sizes = (n_stream, n_span, extent0, extent1, extent2, capacity)
    rows_fwd, rows_bwd, cols_fwd, cols_bwd, weight, column = [jnp.asarray(x) for x in tables]
    operands = [
        coords,
        forces,
        line_id.reshape(1, points),
        line_gain.reshape(1, -1),
        dest_span.reshape(1, points),
        owner_element.reshape(1, points),
        column,
        rows_fwd,
        rows_bwd,
        cols_fwd,
        cols_bwd,
        weight,
        velocity.reshape(3, rows, extent2),
        coefficient.reshape(rows, extent2),
    ]
    outs = pl.pallas_call(
        functools.partial(body, sizes),
        out_shape=(block,) * steps + (jax.ShapeDtypeStruct((1, 1), f32),) * (2 * ITERS + 1),
        in_specs=[hbm] * N_IN,
        out_specs=(hbm,) * steps + (vmem,) * (2 * ITERS + 1),
        scratch_shapes=[pltpu.VMEM(x.shape, x.dtype) for x in operands]
        + [
            pltpu.VMEM((2 * rows, 4 * rows), jnp.bfloat16),
            pltpu.VMEM((rows, 6 * rows), jnp.bfloat16),
            pltpu.VMEM((3 * CHUNK, CHUNK), jnp.bfloat16),
            pltpu.VMEM((3 * CHUNK, CHUNK), jnp.bfloat16),
            pltpu.VMEM((steps, rows, extent2), f32),
            pltpu.VMEM((steps, rows, extent2), f32),
            pltpu.VMEM((rows, extent2), f32),
            pltpu.VMEM((n_span, 8, LANES), f32),
            pltpu.VMEM((n_span, 8, LANES), f32),
            pltpu.VMEM((rows, 2 * total_pts), f32),
            pltpu.VMEM((extent2, 2 * total_pts), f32),
            pltpu.VMEM((steps, 2, extent1, extent2), f32),
            pltpu.VMEM((steps, 2, extent0, extent2), f32),
            pltpu.VMEM((steps, 2, extent0, extent2), f32),
            pltpu.VMEM((steps, 4, 1, extent2), f32),
            pltpu.VMEM((steps, 4, 1, extent2), f32),
            pltpu.VMEM((n_span, 8, LANES), f32),
            pltpu.VMEM((n_stream, 8, LANES), f32),
            pltpu.SemaphoreType.DMA((N_IN,)),
            pltpu.SemaphoreType.DMA((steps,)),
            pltpu.SemaphoreType.DMA((n_span,)),
            pltpu.SemaphoreType.DMA((n_span,)),
            pltpu.SemaphoreType.DMA((steps, 8, PARTS)),
            pltpu.SemaphoreType.DMA((steps, 8, PARTS)),
            pltpu.SemaphoreType.DMA((n_span,)),
            pltpu.SemaphoreType.DMA((n_span,)),
            pltpu.SemaphoreType.DMA((n_stream,)),
            pltpu.SemaphoreType.DMA((n_stream,)),
        ],
        compiler_params=pltpu.CompilerParams(
            collective_id=0, has_side_effects=True, vmem_limit_bytes=60 * 1024 * 1024
        ),
        cost_estimate=pl.CostEstimate(
            flops=6 * 10**9, bytes_accessed=4 * 2**20, transcendentals=10**4
        ),
        name="wind_farm_step",
    )(*operands)
    shape = (extent0, extent1, extent2)
    basis = [vector.reshape(shape) for vector in outs[:steps]]
    factors = [factor.reshape(()) for factor in outs[steps:]]
    pressure = sum(factors[i] * basis[i] for i in range(ITERS))
    residual = sum(factors[ITERS + i] * basis[i] for i in range(steps))
    return pressure, residual


def solution(mesh):
    return jax.shard_map(
        on_device,
        mesh=mesh,
        in_specs=(
            P(None, "stream", "span", None),
            P("stream", "span", None),
            P(None, ("stream", "span")),
            P(None, ("stream", "span")),
            P(("stream", "span")),
            P(),
            P(("stream", "span"), None),
            P(("stream", "span")),
        ),
        out_specs=(P("stream", "span", None), P("stream", "span", None)),
        check_vma=False,
    )
```

```python
import functools

import jax
import jax.numpy as jnp
import numpy as np
from jax import lax
from jax.experimental import pallas as pl
from jax.experimental.pallas import tpu as pltpu
from jax.sharding import PartitionSpec as P

POLY = 8
ITERS = 3
LANES = 128
CHUNK = 256
PARTS = 4
N_IN = 14

kernel_width = 0.45
gll_nodes = [
    -1.0,
    -0.8717401485096066,
    -0.5917001814331423,
    -0.2092992179024789,
    0.2092992179024789,
    0.5917001814331423,
    0.8717401485096066,
    1.0,
]
MESH = pl.DeviceIdType.MESH
OFFSETS = [(1, 0), (-1, 0), (0, 1), (0, -1), (1, 1), (1, -1), (-1, 1), (-1, -1)]


def legendre_value(point, degree):
    previous = 1.0
    current = point
    for order in range(1, degree):
        following = ((2 * order + 1) * point * current - order * previous) / (order + 1)
        previous = current
        current = following
    return current


def gll_tables():
    degree = POLY - 1
    values = [legendre_value(point, degree) for point in gll_nodes]
    weights = [2.0 / (degree * (degree + 1) * value * value) for value in values]
    diffmat = np.zeros((POLY, POLY))
    for i in range(POLY):
        for j in range(POLY):
            if i != j:
                diffmat[i, j] = values[i] / (values[j] * (gll_nodes[i] - gll_nodes[j]))
    diffmat[0, 0] = -degree * (degree + 1) / 4.0
    diffmat[-1, -1] = degree * (degree + 1) / 4.0
    return (
        np.asarray(gll_nodes, np.float32),
        np.asarray(weights, np.float32),
        np.asarray(diffmat, np.float32),
    )


def constants(extent0, extent1):
    nodes, weights, diffmat = gll_tables()
    eye = functools.partial(np.eye, dtype=np.float32)
    along0 = np.kron(eye(extent0 // POLY), np.kron(diffmat, eye(extent1)))
    along1 = np.kron(eye(extent0 * extent1 // POLY), diffmat)
    rows = np.concatenate([along0, along1], axis=0)
    cols = np.kron(eye(CHUNK // POLY), diffmat)

    row_weight = np.kron(np.tile(weights, extent0 // POLY), np.tile(weights, extent1 // POLY))
    row_weight = row_weight.astype(np.float32)
    weight = row_weight[:, None] * np.tile(weights, CHUNK // POLY)[None, :]
    table = np.concatenate([nodes[:, None], weights[:, None], diffmat.T * weights[None, :]], axis=1)
    column = np.repeat(table.T.reshape(-1, 1), LANES, axis=1)
    return rows, rows.T.copy(), cols.T.copy(), cols, weight, column


def split2(value):
    high = value.astype(jnp.bfloat16)
    low = (value - high.astype(jnp.float32)).astype(jnp.bfloat16)
    return high, low


def split3(value):
    high = value.astype(jnp.bfloat16)
    rest = value - high.astype(jnp.float32)
    middle = rest.astype(jnp.bfloat16)
    low = (rest - middle.astype(jnp.float32)).astype(jnp.bfloat16)
    return high, middle, low


def dot(first, second):
    return jnp.dot(first, second, preferred_element_type=jnp.float32)


def dot_nt(first, second):
    return lax.dot_general(
        first, second, (((1,), (1,)), ((), ())), preferred_element_type=jnp.float32
    )


def stacked(value, axis):
    high, low = split2(value)
    return jnp.concatenate([high, low, high], axis=axis)


def combine(first, second, moments, shift):
    total = 0.0
    for i, x in enumerate(first):
        for j, y in enumerate(second):
            total = total + x * y * moments[i + j + shift]
    return total


def body(sizes, *refs):
    n_stream, n_span, extent0, extent1, extent2, capacity = sizes
    n_out = ITERS + 2
    hbm_in, outs = refs[:N_IN], refs[N_IN : N_IN + n_out]
    basis_out, factors = outs[: ITERS + 1], outs[ITERS + 1]
    vmem_in = refs[N_IN + n_out : 2 * N_IN + n_out]
    (
        rows_fwd,
        rows_bwd,
        cols_fwd,
        cols_bwd,
        basis,
        work,
        joined,
        out_pts,
        in_pts,
        lhs_pts,
        rhs_pts,
        recv_stream,
        send_span,
        recv_span,
        send_edge,
        recv_edge,
        sums1,
        sums2,
        load_sem,
        store_sem,
        pts_send,
        pts_recv,
        halo_send,
        halo_recv,
        sum1_send,
        sum1_recv,
        sum2_send,
        sum2_recv,
    ) = refs[2 * N_IN + n_out :]
    (
        coords,
        forces,
        line_id,
        line_gain,
        dest_span,
        owner,
        nodes,
        rows_fwd_f32,
        rows_bwd_f32,
        cols_fwd_f32,
        cols_bwd_f32,
        weight,
        vel,
        metric,
    ) = vmem_in
    rows = extent0 * extent1
    me_s, me_p = lax.axis_index("stream"), lax.axis_index("span")

    def exists(offset):
        s, p = me_s + offset[0], me_p + offset[1]
        return (s >= 0) & (s < n_stream) & (p >= 0) & (p < n_span)

    def at_offset(offset):
        return (
            lax.rem(me_s + offset[0] + n_stream, n_stream),
            lax.rem(me_p + offset[1] + n_span, n_span),
        )

    span_peers = [lax.rem(me_p + j, n_span) for j in range(1, n_span)]
    stream_peers = [lax.rem(me_s + j, n_stream) for j in range(1, n_stream)]

    barrier = pltpu.get_barrier_semaphore()
    for peer in span_peers:
        pl.semaphore_signal(barrier, inc=1, device_id=(me_s, peer), device_id_type=MESH)
    for peer in stream_peers:
        pl.semaphore_signal(barrier, inc=1, device_id=(peer, me_p), device_id_type=MESH)
    greeted = n_span - 1 + n_stream - 1
    for offset in OFFSETS[4:]:

        @pl.when(exists(offset))
        def _(offset=offset):
            pl.semaphore_signal(
                barrier, inc=1, device_id=at_offset(offset), device_id_type=MESH
            )

        greeted = greeted + exists(offset).astype(jnp.int32)

    loads = [
        pltpu.make_async_copy(hbm_in[n], vmem_in[n], load_sem.at[n]) for n in range(N_IN)
    ]
    for load in loads:
        load.start()

    def from_offset(d):
        return exists((-OFFSETS[d][0], -OFFSETS[d][1]))

    for d in range(8):
        buffer = (recv_stream, recv_span, recv_edge)[0 if d < 2 else 1 if d < 4 else 2]
        at = d if d < 2 else d - 2 if d < 4 else d - 4

        @pl.when(jnp.logical_not(from_offset(d)))
        def _(buffer=buffer, at=at):
            for k in range(ITERS + 1):
                buffer[k, at] = jnp.zeros(buffer.shape[2:], jnp.float32)

    points = coords.shape[1]
    group = LANES // capacity
    groups = n_span // group
    lines = line_gain.shape[1]
    earlier = (
        lax.broadcasted_iota(jnp.int32, (points, points), 0)
        < lax.broadcasted_iota(jnp.int32, (points, points), 1)
    ).astype(jnp.bfloat16)
    for load in loads[:7]:
        load.wait()
    ids = line_id[...]
    chosen = (lax.broadcasted_iota(jnp.int32, (lines, points), 0) == ids).astype(jnp.bfloat16)
    gain = sum(dot(part, chosen) for part in reversed(split3(line_gain[...])))
    scaled = forces[...] * gain
    target = dest_span[...]
    spans_at = lax.broadcasted_iota(jnp.int32, (n_span, points), 0)
    named = (spans_at == target).astype(jnp.float32)
    before = dot(named.astype(jnp.bfloat16), earlier)
    rank = jnp.sum(named * before, axis=0, keepdims=True).astype(jnp.int32)
    slot = target * LANES + lax.rem(me_p, group) * capacity + rank
    payload = jnp.concatenate(
        [
            coords[...],
            scaled,
            owner[...].astype(jnp.float32),
            jnp.zeros((1, points), jnp.float32),
        ],
        axis=0,
    )
    parts = jnp.concatenate(
        [p.astype(jnp.float32) for p in split3(payload)], axis=0
    ).astype(jnp.bfloat16)
    for dest in range(n_span):
        placed = (
            lax.broadcasted_iota(jnp.int32, (LANES, points), 0) + dest * LANES == slot
        ).astype(jnp.float32).astype(jnp.bfloat16)
        tile = dot_nt(parts, placed)
        out_pts[dest] = (tile[16:24] + tile[8:16]) + tile[0:8]

    pl.semaphore_wait(barrier, greeted)

    def points_copy(peer, slot_at):
        return pltpu.make_async_remote_copy(
            src_ref=out_pts.at[peer],
            dst_ref=in_pts.at[slot_at],
            send_sem=pts_send.at[peer],
            recv_sem=pts_recv.at[slot_at],
            device_id=(me_s, peer),
            device_id_type=MESH,
        )

    for peer in span_peers:
        points_copy(peer, me_p).start()
    in_pts[me_p] = out_pts[me_p]

    for load in loads[7:12]:
        load.wait()
    high, low = split2(rows_fwd_f32[...])
    rows_fwd[...] = jnp.concatenate([high, high, low, low], axis=1)
    high, low = split2(rows_bwd_f32[...])
    rows_bwd[...] = jnp.concatenate([high, high, low], axis=1)
    for matrix, out in ((cols_fwd_f32, cols_fwd), (cols_bwd_f32, cols_bwd)):
        high, low = split2(matrix[...])
        out[...] = jnp.concatenate([high, high, low], axis=0)

    chunks = [slice(c, c + CHUNK) for c in range(0, extent2, CHUNK)]
    for load in loads[12:]:
        load.wait()
    for cols in chunks:
        w = weight[...]
        both = jnp.concatenate([w * vel[0, :, cols], w * vel[1, :, cols]], axis=0)
        work[0, :, cols] = dot(rows_bwd[...], stacked(both, 0)) + dot(
            stacked(w * vel[2, :, cols], 1), cols_bwd[...]
        )
        metric[:, cols] = metric[:, cols] * w

    for peer in span_peers:
        points_copy(peer, peer).wait_recv()

    elems2 = extent2 // POLY
    total_pts = groups * LANES
    node_col = nodes[0:POLY]
    weight_col = nodes[POLY : 2 * POLY]
    diff_cols = [nodes[(2 + a) * POLY : (3 + a) * POLY] for a in range(POLY)]
    for g in range(groups):
        tile = in_pts[g * group]
        for i in range(1, group):
            tile = tile + in_pts[g * group + i]
        lanes = slice(g * LANES, (g + 1) * LANES)
        lanes_diff = slice(total_pts + g * LANES, total_pts + (g + 1) * LANES)
        plain, diff = [], []
        for k in range(3):
            kern = jnp.exp(-(((node_col - tile[k : k + 1]) / kernel_width) ** 2))
            plain.append(weight_col * kern)
            diff.append(sum(diff_cols[a] * kern[a : a + 1] for a in range(POLY)))
        elem = tile[6:7].astype(jnp.int32)
        elem_y = lax.rem(lax.div(elem, elems2), extent1 // POLY)
        elem_x = lax.div(elem, elems2 * (extent1 // POLY))
        elem_z = lax.rem(elem, elems2)
        for a in range(extent0):
            for ey in range(extent1 // POLY):
                mine = (elem_x == a // POLY) & (elem_y == ey)
                at = slice(a % POLY, a % POLY + 1)
                factor0 = jnp.where(mine, tile[3:4] * diff[0][at], 0.0)
                factor1 = jnp.where(mine, tile[4:5] * plain[0][at], 0.0)
                factor2 = jnp.where(mine, tile[5:6] * plain[0][at], 0.0)
                base = a * extent1 + ey * POLY
                lhs_pts[base : base + POLY, lanes] = factor0 * plain[1] + factor1 * diff[1]
                lhs_pts[base : base + POLY, lanes_diff] = factor2 * plain[1]
        for ez in range(elems2):
            at = slice(ez * POLY, (ez + 1) * POLY)
            rhs_pts[at, lanes] = jnp.where(elem_z == ez, plain[2], 0.0)
            rhs_pts[at, lanes_diff] = jnp.where(elem_z == ez, diff[2], 0.0)

    left_pts = stacked(lhs_pts[...], 1)

    def tile_sum(value):
        total = jnp.sum(value.reshape(rows // POLY, POLY, CHUNK), axis=0)
        return sum(total[:, at : at + LANES] for at in range(0, CHUNK, LANES))

    def rhs_chunk(cols):
        high, low = split2(rhs_pts[cols, :])
        force = dot_nt(left_pts, jnp.concatenate([high, high, low], axis=1))
        work[0, :, cols] = work[0, :, cols] + force

    def operator_chunk(k, cols):
        field = basis[k, :, cols]
        high, low = split2(field)
        m = metric[:, cols]
        grad = dot(rows_fwd[...], jnp.concatenate([high, low, high, low], axis=0))
        grad2 = dot(jnp.concatenate([high, low, high], axis=1), cols_fwd[...])
        both = jnp.concatenate([grad[:rows] * m, grad[rows:] * m], axis=0)
        out = (
            dot(rows_bwd[...], stacked(both, 0))
            + dot(stacked(grad2 * m, 1), cols_bwd[...])
            + weight[...] * field
        )
        work[k + 1, :, cols] = out
        return tile_sum(field * work[k, :, cols]), tile_sum(field * out)

    last0, last1 = extent0 - 1, extent1 - 1
    part_width = extent2 // PARTS

    def halo_copy(k, d, q):
        cols = pl.ds(q * part_width, part_width)
        if d < 2:
            src = work.at[k, pl.ds(last0 * extent1 if d == 0 else 0, extent1), cols]
            dst = recv_stream.at[k, d, :, cols]
        elif d < 4:
            src, dst = send_span.at[k, d - 2, :, cols], recv_span.at[k, d - 2, :, cols]
        else:
            src, dst = send_edge.at[k, d - 4, :, cols], recv_edge.at[k, d - 4, :, cols]
        return pltpu.make_async_remote_copy(
            src_ref=src,
            dst_ref=dst,
            send_sem=halo_send.at[k, d, q],
            recv_sem=halo_recv.at[k, d, q],
            device_id=at_offset(OFFSETS[d]),
            device_id_type=MESH,
        )

    def send_faces(k, q):
        cols = slice(q * part_width, (q + 1) * part_width)
        for a in range(extent0):
            top = work[k, a * extent1 + last1 : a * extent1 + last1 + 1, cols]
            bottom = work[k, a * extent1 : a * extent1 + 1, cols]
            send_span[k, 0, a : a + 1, cols] = top
            send_span[k, 1, a : a + 1, cols] = bottom
            if a == last0:
                send_edge[k, 0, :, cols] = top
                send_edge[k, 1, :, cols] = bottom
            if a == 0:
                send_edge[k, 2, :, cols] = top
                send_edge[k, 3, :, cols] = bottom
        for d in range(8):

            @pl.when(exists(OFFSETS[d]))
            def _(d=d):
                halo_copy(k, d, q).start()

    def join(k, q):
        for d in (2, 3, 4, 5, 6, 7, 0, 1):

            @pl.when(from_offset(d))
            def _(d=d):
                halo_copy(k, d, q).wait_recv()

        cols = slice(q * part_width, (q + 1) * part_width)
        sub = lax.broadcasted_iota(jnp.int32, (POLY, part_width), 0)
        for a in range(extent0):
            tiles = []
            for ey in range(extent1 // POLY):
                base = a * extent1 + ey * POLY
                x = work[k, base : base + POLY, cols]
                if a == 0:
                    x = x + recv_stream[k, 0, ey * POLY : (ey + 1) * POLY, cols]
                if a == last0:
                    x = x + recv_stream[k, 1, ey * POLY : (ey + 1) * POLY, cols]
                tiles.append(x)
            lower = recv_span[k, 0, a : a + 1, cols]
            upper = recv_span[k, 1, a : a + 1, cols]
            if a == 0:
                lower = lower + recv_edge[k, 0, :, cols]
                upper = upper + recv_edge[k, 1, :, cols]
            if a == last0:
                lower = lower + recv_edge[k, 2, :, cols]
                upper = upper + recv_edge[k, 3, :, cols]
            for ey, x in enumerate(tiles):
                below = lower if ey == 0 else pltpu.roll(tiles[ey - 1], 1, 0)
                above = upper if ey + 1 == len(tiles) else pltpu.roll(tiles[ey + 1], POLY - 1, 0)
                base = a * extent1 + ey * POLY
                joined[base : base + POLY, cols] = (
                    x + jnp.where(sub == 0, below, 0.0) + jnp.where(sub == POLY - 1, above, 0.0)
                )

    def assemble(k, cols):
        start, stop = max(cols.start - LANES, 0), min(cols.stop + LANES, extent2)
        width = stop - start
        lane = lax.broadcasted_iota(jnp.int32, (POLY, CHUNK), 1) + cols.start
        first2 = (lane % POLY == 0) & (lane > 0)
        last2 = (lane % POLY == POLY - 1) & (lane < extent2 - 1)
        inner = slice(cols.start - start, cols.stop - start)
        for base in range(0, rows, POLY):
            x = joined[base : base + POLY, start:stop]
            lower = pltpu.roll(x, 1, 1)[:, inner]
            upper = pltpu.roll(x, width - 1, 1)[:, inner]
            basis[k, base : base + POLY, cols] = (
                x[:, inner] + jnp.where(first2, lower, 0.0) + jnp.where(last2, upper, 0.0)
            )

    per_part = len(chunks) // PARTS

    def store(k):
        return pltpu.make_async_copy(basis.at[k], basis_out[k], store_sem.at[k])

    def joined_chunks(k):
        have = 0
        for n, cols in enumerate(chunks):
            need = min((n + 1) // per_part + 1, PARTS)
            while have < need:
                join(k, have)
                have += 1
            assemble(k, cols)
            if n + 1 == len(chunks):
                store(k).start()
            yield n, cols

    for n, cols in enumerate(chunks):
        rhs_chunk(cols)
        if (n + 1) % per_part == 0:
            send_faces(0, n // per_part)
    mine = []
    for k in range(ITERS):
        even = odd = 0.0
        for n, cols in joined_chunks(k):
            more = operator_chunk(k, cols)
            even, odd = even + more[0], odd + more[1]
            if (n + 1) % per_part == 0:
                send_faces(k + 1, n // per_part)
        mine += [even, odd]

    mine = [jnp.sum(total, axis=0, keepdims=True) for total in mine]
    mine.append(jnp.zeros((8 - len(mine), LANES), jnp.float32))
    sums1[me_p] = jnp.concatenate(mine, axis=0)

    def sum1_copy(peer, slot_at):
        return pltpu.make_async_remote_copy(
            src_ref=sums1.at[me_p],
            dst_ref=sums1.at[slot_at],
            send_sem=sum1_send.at[peer],
            recv_sem=sum1_recv.at[slot_at],
            device_id=(me_s, peer),
            device_id_type=MESH,
        )

    def sum2_copy(peer, slot_at):
        return pltpu.make_async_remote_copy(
            src_ref=sums2.at[me_s],
            dst_ref=sums2.at[slot_at],
            send_sem=sum2_send.at[peer],
            recv_sem=sum2_recv.at[slot_at],
            device_id=(peer, me_p),
            device_id_type=MESH,
        )

    for peer in span_peers:
        sum1_copy(peer, me_p).start()
    for peer in span_peers:
        sum1_copy(peer, peer).wait_recv()
    total = sums1[0]
    for i in range(1, n_span):
        total = total + sums1[i]
    sums2[me_s] = total
    for peer in stream_peers:
        sum2_copy(peer, me_s).start()
    for _ in joined_chunks(ITERS):
        pass
    for peer in stream_peers:
        sum2_copy(peer, peer).wait_recv()
    total = sums2[0]
    for i in range(1, n_stream):
        total = total + sums2[i]
    total = jnp.broadcast_to(jnp.sum(total, axis=1, keepdims=True), (8, LANES))
    moments = [total[n : n + 1] for n in range(2 * ITERS)]

    one = jnp.ones((1, LANES), jnp.float32)
    res, direction, pres = [one], [one], [0.0] * ITERS
    norm = moments[0]
    for iteration in range(ITERS):
        step_len = norm / combine(direction, direction, moments, 1)
        for i, x in enumerate(direction):
            pres[i] = pres[i] + step_len * x
        res = res + [0.0]
        res = [res[0]] + [x - step_len * y for x, y in zip(res[1:], direction)]
        if iteration + 1 < ITERS:
            norm_next = combine(res, res, moments, 0)
            ratio = norm_next / norm
            direction = [x + ratio * y for x, y in zip(res, direction + [0.0])]
            norm = norm_next

    factors[...] = jnp.concatenate(pres + res + [jnp.zeros((1, LANES), jnp.float32)], axis=0)

    for k in range(ITERS + 1):
        store(k).wait()
    for peer in span_peers:
        points_copy(peer, me_p).wait_send()
        sum1_copy(peer, me_p).wait_send()
    for peer in stream_peers:
        sum2_copy(peer, me_s).wait_send()
    for d in range(8):

        @pl.when(exists(OFFSETS[d]))
        def _(d=d):
            for k in range(ITERS + 1):
                for q in range(PARTS):
                    halo_copy(k, d, q).wait_send()


def outputs_body(pieces, *refs):
    steps = ITERS + 1
    basis_in, factors_in, outs = refs[:steps], refs[steps], refs[steps + 1 : steps + 3]
    factors, basis, made, load_sem, store_sem = refs[steps + 3 :]
    rows, width = basis.shape[1:]
    height = rows // pieces
    first = pltpu.make_async_copy(factors_in, factors, load_sem.at[pieces * steps])
    first.start()

    def load(n, i):
        at = pl.ds(n * height, height)
        return pltpu.make_async_copy(
            basis_in[i].at[at], basis.at[i, at], load_sem.at[n * steps + i]
        )

    def store(n, i):
        at = pl.ds(n * height, height)
        return pltpu.make_async_copy(made.at[i, at], outs[i].at[at], store_sem.at[n * 2 + i])

    for n in range(pieces):
        for i in range(steps):
            load(n, i).start()
    first.wait()
    rates = [jnp.broadcast_to(factors[i : i + 1, 0:1], (POLY, width)) for i in range(2 * ITERS + 1)]
    for n in range(pieces):
        for i in range(steps):
            load(n, i).wait()
        for base in range(n * height, (n + 1) * height, POLY):
            at = slice(base, base + POLY)
            vec = [basis[i, at, :] for i in range(steps)]
            made[0, at, :] = sum(rates[i] * vec[i] for i in range(ITERS))
            made[1, at, :] = sum(rates[ITERS + i] * vec[i] for i in range(steps))
        for i in range(2):
            store(n, i).start()
    for n in range(pieces):
        for i in range(2):
            store(n, i).wait()


def on_device(velocity, coefficient, coords, forces, line_id, line_gain, dest_span, owner_element):
    extent0, extent1, extent2 = coefficient.shape
    rows = extent0 * extent1
    points = coords.shape[1]
    n_stream, n_span = lax.axis_size("stream"), lax.axis_size("span")
    capacity = max(2, 2 * points // n_span)
    total_pts = n_span * capacity
    tables = constants(extent0, extent1)
    f32 = jnp.float32
    block = jax.ShapeDtypeStruct((rows, extent2), f32)
    vmem = pl.BlockSpec(memory_space=pltpu.VMEM)
    hbm = pl.BlockSpec(memory_space=pl.ANY)
    steps = ITERS + 1
    sizes = (n_stream, n_span, extent0, extent1, extent2, capacity)
    rows_fwd, rows_bwd, cols_fwd, cols_bwd, weight, column = [jnp.asarray(x) for x in tables]
    operands = [
        coords,
        forces,
        line_id.reshape(1, points),
        line_gain.reshape(1, -1),
        dest_span.reshape(1, points),
        owner_element.reshape(1, points),
        column,
        rows_fwd,
        rows_bwd,
        cols_fwd,
        cols_bwd,
        weight,
        velocity.reshape(3, rows, extent2),
        coefficient.reshape(rows, extent2),
    ]
    outs = pl.pallas_call(
        functools.partial(body, sizes),
        out_shape=(block,) * steps + (jax.ShapeDtypeStruct((8, LANES), f32),),
        in_specs=[hbm] * N_IN,
        out_specs=(hbm,) * steps + (vmem,),
        scratch_shapes=[pltpu.VMEM(x.shape, x.dtype) for x in operands]
        + [
            pltpu.VMEM((2 * rows, 4 * rows), jnp.bfloat16),
            pltpu.VMEM((rows, 6 * rows), jnp.bfloat16),
            pltpu.VMEM((3 * CHUNK, CHUNK), jnp.bfloat16),
            pltpu.VMEM((3 * CHUNK, CHUNK), jnp.bfloat16),
            pltpu.VMEM((steps, rows, extent2), f32),
            pltpu.VMEM((steps, rows, extent2), f32),
            pltpu.VMEM((rows, extent2), f32),
            pltpu.VMEM((n_span, 8, LANES), f32),
            pltpu.VMEM((n_span, 8, LANES), f32),
            pltpu.VMEM((rows, 2 * total_pts), f32),
            pltpu.VMEM((extent2, 2 * total_pts), f32),
            pltpu.VMEM((steps, 2, extent1, extent2), f32),
            pltpu.VMEM((steps, 2, extent0, extent2), f32),
            pltpu.VMEM((steps, 2, extent0, extent2), f32),
            pltpu.VMEM((steps, 4, 1, extent2), f32),
            pltpu.VMEM((steps, 4, 1, extent2), f32),
            pltpu.VMEM((n_span, 8, LANES), f32),
            pltpu.VMEM((n_stream, 8, LANES), f32),
            pltpu.SemaphoreType.DMA((N_IN,)),
            pltpu.SemaphoreType.DMA((steps,)),
            pltpu.SemaphoreType.DMA((n_span,)),
            pltpu.SemaphoreType.DMA((n_span,)),
            pltpu.SemaphoreType.DMA((steps, 8, PARTS)),
            pltpu.SemaphoreType.DMA((steps, 8, PARTS)),
            pltpu.SemaphoreType.DMA((n_span,)),
            pltpu.SemaphoreType.DMA((n_span,)),
            pltpu.SemaphoreType.DMA((n_stream,)),
            pltpu.SemaphoreType.DMA((n_stream,)),
        ],
        compiler_params=pltpu.CompilerParams(
            collective_id=0, has_side_effects=True, vmem_limit_bytes=60 * 1024 * 1024
        ),
        cost_estimate=pl.CostEstimate(
            flops=6 * 10**9, bytes_accessed=4 * 2**20, transcendentals=10**4
        ),
        name="wind_farm_step",
    )(*operands)
    pieces = 4
    pressure, residual = pl.pallas_call(
        functools.partial(outputs_body, pieces),
        out_shape=(block, block),
        in_specs=[hbm] * (steps + 1),
        out_specs=(hbm, hbm),
        scratch_shapes=[
            pltpu.VMEM((8, LANES), f32),
            pltpu.VMEM((steps, rows, extent2), f32),
            pltpu.VMEM((2, rows, extent2), f32),
            pltpu.SemaphoreType.DMA((1 + pieces * steps,)),
            pltpu.SemaphoreType.DMA((pieces * 2,)),
        ],
        compiler_params=pltpu.CompilerParams(vmem_limit_bytes=60 * 1024 * 1024),
        name="outputs",
    )(*outs)
    shape = (extent0, extent1, extent2)
    return pressure.reshape(shape), residual.reshape(shape)


def solution(mesh):
    return jax.shard_map(
        on_device,
        mesh=mesh,
        in_specs=(
            P(None, "stream", "span", None),
            P("stream", "span", None),
            P(None, ("stream", "span")),
            P(None, ("stream", "span")),
            P(("stream", "span")),
            P(),
            P(("stream", "span"), None),
            P(("stream", "span")),
        ),
        out_specs=(P("stream", "span", None), P("stream", "span", None)),
        check_vma=False,
    )
```

```python
import functools

import jax
import jax.numpy as jnp
import numpy as np
from jax import lax
from jax.experimental import pallas as pl
from jax.experimental.pallas import tpu as pltpu
from jax.sharding import PartitionSpec as P

POLY = 8
ITERS = 3
LANES = 128
CHUNK = 256
PARTS = 2
N_IN = 14

kernel_width = 0.45
gll_nodes = [
    -1.0,
    -0.8717401485096066,
    -0.5917001814331423,
    -0.2092992179024789,
    0.2092992179024789,
    0.5917001814331423,
    0.8717401485096066,
    1.0,
]
MESH = pl.DeviceIdType.MESH
OFFSETS = [(1, 0), (-1, 0), (0, 1), (0, -1), (1, 1), (1, -1), (-1, 1), (-1, -1)]


def legendre_value(point, degree):
    previous = 1.0
    current = point
    for order in range(1, degree):
        following = ((2 * order + 1) * point * current - order * previous) / (order + 1)
        previous = current
        current = following
    return current


def gll_tables():
    degree = POLY - 1
    values = [legendre_value(point, degree) for point in gll_nodes]
    weights = [2.0 / (degree * (degree + 1) * value * value) for value in values]
    diffmat = np.zeros((POLY, POLY))
    for i in range(POLY):
        for j in range(POLY):
            if i != j:
                diffmat[i, j] = values[i] / (values[j] * (gll_nodes[i] - gll_nodes[j]))
    diffmat[0, 0] = -degree * (degree + 1) / 4.0
    diffmat[-1, -1] = degree * (degree + 1) / 4.0
    return (
        np.asarray(gll_nodes, np.float32),
        np.asarray(weights, np.float32),
        np.asarray(diffmat, np.float32),
    )


def constants(extent0, extent1):
    nodes, weights, diffmat = gll_tables()
    eye = functools.partial(np.eye, dtype=np.float32)
    along0 = np.kron(eye(extent0 // POLY), np.kron(diffmat, eye(extent1)))
    along1 = np.kron(eye(extent0 * extent1 // POLY), diffmat)
    rows = np.concatenate([along0, along1], axis=0)
    cols = np.kron(eye(CHUNK // POLY), diffmat)

    row_weight = np.kron(np.tile(weights, extent0 // POLY), np.tile(weights, extent1 // POLY))
    row_weight = row_weight.astype(np.float32)
    weight = row_weight[:, None] * np.tile(weights, CHUNK // POLY)[None, :]
    table = np.concatenate([nodes[:, None], weights[:, None], diffmat.T * weights[None, :]], axis=1)
    column = np.repeat(table.T.reshape(-1, 1), LANES, axis=1)
    return rows, rows.T.copy(), cols.T.copy(), cols, weight, column


def split2(value):
    high = value.astype(jnp.bfloat16)
    low = (value - high.astype(jnp.float32)).astype(jnp.bfloat16)
    return high, low


def split3(value):
    high = value.astype(jnp.bfloat16)
    rest = value - high.astype(jnp.float32)
    middle = rest.astype(jnp.bfloat16)
    low = (rest - middle.astype(jnp.float32)).astype(jnp.bfloat16)
    return high, middle, low


def dot(first, second):
    return jnp.dot(first, second, preferred_element_type=jnp.float32)


def dot_nt(first, second):
    return lax.dot_general(
        first, second, (((1,), (1,)), ((), ())), preferred_element_type=jnp.float32
    )


def stacked(value, axis):
    high, low = split2(value)
    return jnp.concatenate([high, low, high], axis=axis)


def combine(first, second, moments, shift):
    total = 0.0
    for i, x in enumerate(first):
        for j, y in enumerate(second):
            total = total + x * y * moments[i + j + shift]
    return total


def body(sizes, *refs):
    n_stream, n_span, extent0, extent1, extent2, capacity = sizes
    n_out = ITERS + 2
    hbm_in, outs = refs[:N_IN], refs[N_IN : N_IN + n_out]
    basis_out, factors = outs[: ITERS + 1], outs[ITERS + 1]
    vmem_in = refs[N_IN + n_out : 2 * N_IN + n_out]
    (
        rows_fwd,
        rows_bwd,
        cols_fwd,
        cols_bwd,
        basis,
        work,
        joined,
        out_pts,
        in_pts,
        lhs_pts,
        rhs_pts,
        recv_stream,
        send_span,
        recv_span,
        send_edge,
        recv_edge,
        sums1,
        sums2,
        load_sem,
        store_sem,
        pts_send,
        pts_recv,
        halo_send,
        halo_recv,
        sum1_send,
        sum1_recv,
        sum2_send,
        sum2_recv,
    ) = refs[2 * N_IN + n_out :]
    (
        coords,
        forces,
        line_id,
        line_gain,
        dest_span,
        owner,
        nodes,
        rows_fwd_f32,
        rows_bwd_f32,
        cols_fwd_f32,
        cols_bwd_f32,
        weight,
        vel,
        metric,
    ) = vmem_in
    rows = extent0 * extent1
    me_s, me_p = lax.axis_index("stream"), lax.axis_index("span")

    def exists(offset):
        s, p = me_s + offset[0], me_p + offset[1]
        return (s >= 0) & (s < n_stream) & (p >= 0) & (p < n_span)

    def at_offset(offset):
        return (
            lax.rem(me_s + offset[0] + n_stream, n_stream),
            lax.rem(me_p + offset[1] + n_span, n_span),
        )

    span_peers = [lax.rem(me_p + j, n_span) for j in range(1, n_span)]
    stream_peers = [lax.rem(me_s + j, n_stream) for j in range(1, n_stream)]

    barrier = pltpu.get_barrier_semaphore()
    for peer in span_peers:
        pl.semaphore_signal(barrier, inc=1, device_id=(me_s, peer), device_id_type=MESH)
    for peer in stream_peers:
        pl.semaphore_signal(barrier, inc=1, device_id=(peer, me_p), device_id_type=MESH)
    greeted = n_span - 1 + n_stream - 1
    for offset in OFFSETS[4:]:

        @pl.when(exists(offset))
        def _(offset=offset):
            pl.semaphore_signal(
                barrier, inc=1, device_id=at_offset(offset), device_id_type=MESH
            )

        greeted = greeted + exists(offset).astype(jnp.int32)

    loads = [
        pltpu.make_async_copy(hbm_in[n], vmem_in[n], load_sem.at[n]) for n in range(N_IN)
    ]
    for load in loads:
        load.start()

    def from_offset(d):
        return exists((-OFFSETS[d][0], -OFFSETS[d][1]))

    for d in range(8):
        buffer = (recv_stream, recv_span, recv_edge)[0 if d < 2 else 1 if d < 4 else 2]
        at = d if d < 2 else d - 2 if d < 4 else d - 4

        @pl.when(jnp.logical_not(from_offset(d)))
        def _(buffer=buffer, at=at):
            for k in range(ITERS + 1):
                buffer[k, at] = jnp.zeros(buffer.shape[2:], jnp.float32)

    points = coords.shape[1]
    group = LANES // capacity
    groups = n_span // group
    lines = line_gain.shape[1]
    earlier = (
        lax.broadcasted_iota(jnp.int32, (points, points), 0)
        < lax.broadcasted_iota(jnp.int32, (points, points), 1)
    ).astype(jnp.bfloat16)
    for load in loads[:7]:
        load.wait()
    ids = line_id[...]
    chosen = (lax.broadcasted_iota(jnp.int32, (lines, points), 0) == ids).astype(jnp.bfloat16)
    gain = sum(dot(part, chosen) for part in reversed(split3(line_gain[...])))
    scaled = forces[...] * gain
    target = dest_span[...]
    spans_at = lax.broadcasted_iota(jnp.int32, (n_span, points), 0)
    named = (spans_at == target).astype(jnp.float32)
    before = dot(named.astype(jnp.bfloat16), earlier)
    rank = jnp.sum(named * before, axis=0, keepdims=True).astype(jnp.int32)
    slot = target * LANES + lax.rem(me_p, group) * capacity + rank
    payload = jnp.concatenate(
        [
            coords[...],
            scaled,
            owner[...].astype(jnp.float32),
            jnp.zeros((1, points), jnp.float32),
        ],
        axis=0,
    )
    parts = jnp.concatenate(
        [p.astype(jnp.float32) for p in split3(payload)], axis=0
    ).astype(jnp.bfloat16)
    for dest in range(n_span):
        placed = (
            lax.broadcasted_iota(jnp.int32, (LANES, points), 0) + dest * LANES == slot
        ).astype(jnp.float32).astype(jnp.bfloat16)
        tile = dot_nt(parts, placed)
        out_pts[dest] = (tile[16:24] + tile[8:16]) + tile[0:8]

    pl.semaphore_wait(barrier, greeted)

    def points_copy(peer, slot_at):
        return pltpu.make_async_remote_copy(
            src_ref=out_pts.at[peer],
            dst_ref=in_pts.at[slot_at],
            send_sem=pts_send.at[peer],
            recv_sem=pts_recv.at[slot_at],
            device_id=(me_s, peer),
            device_id_type=MESH,
        )

    for peer in span_peers:
        points_copy(peer, me_p).start()
    in_pts[me_p] = out_pts[me_p]

    for load in loads[7:12]:
        load.wait()
    high, low = split2(rows_fwd_f32[...])
    rows_fwd[...] = jnp.concatenate([high, high, low, low], axis=1)
    high, low = split2(rows_bwd_f32[...])
    rows_bwd[...] = jnp.concatenate([high, high, low], axis=1)
    for matrix, out in ((cols_fwd_f32, cols_fwd), (cols_bwd_f32, cols_bwd)):
        high, low = split2(matrix[...])
        out[...] = jnp.concatenate([high, high, low], axis=0)

    chunks = [slice(c, c + CHUNK) for c in range(0, extent2, CHUNK)]
    for load in loads[12:]:
        load.wait()
    part_width = extent2 // PARTS
    groups_at = [slice(c.start, c.stop) for c in chunks[: len(chunks) // PARTS]]
    for start in range(part_width, extent2, part_width):
        groups_at.append(slice(start, start + part_width))

    def weight_over(cols):
        return jnp.concatenate([weight[...]] * ((cols.stop - cols.start) // CHUNK), axis=1)

    def times_cols(value, matrix):
        count = value.shape[1] // CHUNK
        tall = jnp.concatenate(
            [value[:, i * CHUNK : (i + 1) * CHUNK] for i in range(count)], axis=0
        )
        tall = dot(stacked(tall, 1), matrix[...])
        return jnp.concatenate([tall[i * rows : (i + 1) * rows] for i in range(count)], axis=1)

    for start in range(0, extent2, part_width):
        cols = slice(start, start + part_width)
        w = weight_over(cols)
        both = jnp.concatenate([w * vel[0, :, cols], w * vel[1, :, cols]], axis=0)
        work[0, :, cols] = dot(rows_bwd[...], stacked(both, 0)) + times_cols(
            w * vel[2, :, cols], cols_bwd
        )
        metric[:, cols] = metric[:, cols] * w

    for peer in span_peers:
        points_copy(peer, peer).wait_recv()

    elems2 = extent2 // POLY
    total_pts = groups * LANES
    node_col = nodes[0:POLY]
    weight_col = nodes[POLY : 2 * POLY]
    diff_cols = [nodes[(2 + a) * POLY : (3 + a) * POLY] for a in range(POLY)]
    for g in range(groups):
        tile = in_pts[g * group]
        for i in range(1, group):
            tile = tile + in_pts[g * group + i]
        lanes = slice(g * LANES, (g + 1) * LANES)
        lanes_diff = slice(total_pts + g * LANES, total_pts + (g + 1) * LANES)
        plain, diff = [], []
        for k in range(3):
            kern = jnp.exp(-(((node_col - tile[k : k + 1]) / kernel_width) ** 2))
            plain.append(weight_col * kern)
            diff.append(sum(diff_cols[a] * kern[a : a + 1] for a in range(POLY)))
        elem = tile[6:7].astype(jnp.int32)
        elem_y = lax.rem(lax.div(elem, elems2), extent1 // POLY)
        elem_x = lax.div(elem, elems2 * (extent1 // POLY))
        elem_z = lax.rem(elem, elems2)
        for a in range(extent0):
            for ey in range(extent1 // POLY):
                mine = (elem_x == a // POLY) & (elem_y == ey)
                at = slice(a % POLY, a % POLY + 1)
                factor0 = jnp.where(mine, tile[3:4] * diff[0][at], 0.0)
                factor1 = jnp.where(mine, tile[4:5] * plain[0][at], 0.0)
                factor2 = jnp.where(mine, tile[5:6] * plain[0][at], 0.0)
                base = a * extent1 + ey * POLY
                lhs_pts[base : base + POLY, lanes] = factor0 * plain[1] + factor1 * diff[1]
                lhs_pts[base : base + POLY, lanes_diff] = factor2 * plain[1]
        for ez in range(elems2):
            at = slice(ez * POLY, (ez + 1) * POLY)
            rhs_pts[at, lanes] = jnp.where(elem_z == ez, plain[2], 0.0)
            rhs_pts[at, lanes_diff] = jnp.where(elem_z == ez, diff[2], 0.0)

    left_pts = stacked(lhs_pts[...], 1)

    def tile_sum(value):
        total = jnp.sum(value.reshape(rows // POLY, POLY, value.shape[1]), axis=0)
        return sum(total[:, at : at + LANES] for at in range(0, value.shape[1], LANES))

    def rhs_chunk(cols):
        high, low = split2(rhs_pts[cols, :])
        force = dot_nt(left_pts, jnp.concatenate([high, high, low], axis=1))
        work[0, :, cols] = work[0, :, cols] + force

    def operator_group(k, cols):
        field = basis[k, :, cols]
        high, low = split2(field)
        m = metric[:, cols]
        grad = dot(rows_fwd[...], jnp.concatenate([high, low, high, low], axis=0))
        grad2 = times_cols(field, cols_fwd)
        both = jnp.concatenate([grad[:rows] * m, grad[rows:] * m], axis=0)
        out = (
            dot(rows_bwd[...], stacked(both, 0))
            + times_cols(grad2 * m, cols_bwd)
            + weight_over(cols) * field
        )
        work[k + 1, :, cols] = out
        return tile_sum(field * work[k, :, cols]), tile_sum(field * out)

    last0, last1 = extent0 - 1, extent1 - 1

    def halo_copy(k, d, q):
        cols = pl.ds(q * part_width, part_width)
        if d < 2:
            src = work.at[k, pl.ds(last0 * extent1 if d == 0 else 0, extent1), cols]
            dst = recv_stream.at[k, d, :, cols]
        elif d < 4:
            src, dst = send_span.at[k, d - 2, :, cols], recv_span.at[k, d - 2, :, cols]
        else:
            src, dst = send_edge.at[k, d - 4, :, cols], recv_edge.at[k, d - 4, :, cols]
        return pltpu.make_async_remote_copy(
            src_ref=src,
            dst_ref=dst,
            send_sem=halo_send.at[k, d, q],
            recv_sem=halo_recv.at[k, d, q],
            device_id=at_offset(OFFSETS[d]),
            device_id_type=MESH,
        )

    def send_faces(k, q):
        cols = slice(q * part_width, (q + 1) * part_width)
        for a in range(extent0):
            top = work[k, a * extent1 + last1 : a * extent1 + last1 + 1, cols]
            bottom = work[k, a * extent1 : a * extent1 + 1, cols]
            send_span[k, 0, a : a + 1, cols] = top
            send_span[k, 1, a : a + 1, cols] = bottom
            if a == last0:
                send_edge[k, 0, :, cols] = top
                send_edge[k, 1, :, cols] = bottom
            if a == 0:
                send_edge[k, 2, :, cols] = top
                send_edge[k, 3, :, cols] = bottom
        for d in range(8):

            @pl.when(exists(OFFSETS[d]))
            def _(d=d):
                halo_copy(k, d, q).start()

    def join(k, q):
        for d in (2, 3, 4, 5, 6, 7, 0, 1):

            @pl.when(from_offset(d))
            def _(d=d):
                halo_copy(k, d, q).wait_recv()

        cols = slice(q * part_width, (q + 1) * part_width)
        sub = lax.broadcasted_iota(jnp.int32, (POLY, part_width), 0)
        for a in range(extent0):
            tiles = []
            for ey in range(extent1 // POLY):
                base = a * extent1 + ey * POLY
                x = work[k, base : base + POLY, cols]
                if a == 0:
                    x = x + recv_stream[k, 0, ey * POLY : (ey + 1) * POLY, cols]
                if a == last0:
                    x = x + recv_stream[k, 1, ey * POLY : (ey + 1) * POLY, cols]
                tiles.append(x)
            lower = recv_span[k, 0, a : a + 1, cols]
            upper = recv_span[k, 1, a : a + 1, cols]
            if a == 0:
                lower = lower + recv_edge[k, 0, :, cols]
                upper = upper + recv_edge[k, 1, :, cols]
            if a == last0:
                lower = lower + recv_edge[k, 2, :, cols]
                upper = upper + recv_edge[k, 3, :, cols]
            for ey, x in enumerate(tiles):
                below = lower if ey == 0 else pltpu.roll(tiles[ey - 1], 1, 0)
                above = upper if ey + 1 == len(tiles) else pltpu.roll(tiles[ey + 1], POLY - 1, 0)
                base = a * extent1 + ey * POLY
                joined[base : base + POLY, cols] = (
                    x + jnp.where(sub == 0, below, 0.0) + jnp.where(sub == POLY - 1, above, 0.0)
                )

    def assemble(k, cols):
        start, stop = max(cols.start - LANES, 0), min(cols.stop + LANES, extent2)
        width = stop - start
        lane = lax.broadcasted_iota(jnp.int32, (POLY, CHUNK), 1) + cols.start
        first2 = (lane % POLY == 0) & (lane > 0)
        last2 = (lane % POLY == POLY - 1) & (lane < extent2 - 1)
        inner = slice(cols.start - start, cols.stop - start)
        for base in range(0, rows, POLY):
            x = joined[base : base + POLY, start:stop]
            lower = pltpu.roll(x, 1, 1)[:, inner]
            upper = pltpu.roll(x, width - 1, 1)[:, inner]
            basis[k, base : base + POLY, cols] = (
                x[:, inner] + jnp.where(first2, lower, 0.0) + jnp.where(last2, upper, 0.0)
            )

    def store(k):
        return pltpu.make_async_copy(basis.at[k], basis_out[k], store_sem.at[k])

    def joined_groups(k):
        have = 0
        for cols in groups_at:
            need = min(cols.stop // part_width + 1, PARTS)
            while have < need:
                join(k, have)
                have += 1
            for start in range(cols.start, cols.stop, CHUNK):
                assemble(k, slice(start, start + CHUNK))
            if cols.stop == extent2:
                store(k).start()
            yield cols

    for cols in chunks:
        rhs_chunk(cols)
        if cols.stop % part_width == 0:
            send_faces(0, cols.stop // part_width - 1)
    mine = []
    for k in range(ITERS):
        even = odd = 0.0
        for cols in joined_groups(k):
            more = operator_group(k, cols)
            even, odd = even + more[0], odd + more[1]
            if cols.stop % part_width == 0:
                send_faces(k + 1, cols.stop // part_width - 1)
        mine += [even, odd]

    mine = [jnp.sum(total, axis=0, keepdims=True) for total in mine]
    mine.append(jnp.zeros((8 - len(mine), LANES), jnp.float32))
    sums1[me_p] = jnp.concatenate(mine, axis=0)

    def sum1_copy(peer, slot_at):
        return pltpu.make_async_remote_copy(
            src_ref=sums1.at[me_p],
            dst_ref=sums1.at[slot_at],
            send_sem=sum1_send.at[peer],
            recv_sem=sum1_recv.at[slot_at],
            device_id=(me_s, peer),
            device_id_type=MESH,
        )

    def sum2_copy(peer, slot_at):
        return pltpu.make_async_remote_copy(
            src_ref=sums2.at[me_s],
            dst_ref=sums2.at[slot_at],
            send_sem=sum2_send.at[peer],
            recv_sem=sum2_recv.at[slot_at],
            device_id=(peer, me_p),
            device_id_type=MESH,
        )

    for peer in span_peers:
        sum1_copy(peer, me_p).start()
    for peer in span_peers:
        sum1_copy(peer, peer).wait_recv()
    total = sums1[0]
    for i in range(1, n_span):
        total = total + sums1[i]
    sums2[me_s] = total
    for peer in stream_peers:
        sum2_copy(peer, me_s).start()
    for _ in joined_groups(ITERS):
        pass
    for peer in stream_peers:
        sum2_copy(peer, peer).wait_recv()
    total = sums2[0]
    for i in range(1, n_stream):
        total = total + sums2[i]
    total = jnp.broadcast_to(jnp.sum(total, axis=1, keepdims=True), (8, LANES))
    moments = [total[n : n + 1] for n in range(2 * ITERS)]

    one = jnp.ones((1, LANES), jnp.float32)
    res, direction, pres = [one], [one], [0.0] * ITERS
    norm = moments[0]
    for iteration in range(ITERS):
        step_len = norm / combine(direction, direction, moments, 1)
        for i, x in enumerate(direction):
            pres[i] = pres[i] + step_len * x
        res = res + [0.0]
        res = [res[0]] + [x - step_len * y for x, y in zip(res[1:], direction)]
        if iteration + 1 < ITERS:
            norm_next = combine(res, res, moments, 0)
            ratio = norm_next / norm
            direction = [x + ratio * y for x, y in zip(res, direction + [0.0])]
            norm = norm_next

    factors[...] = jnp.concatenate(pres + res + [jnp.zeros((1, LANES), jnp.float32)], axis=0)

    for k in range(ITERS + 1):
        store(k).wait()
    for peer in span_peers:
        points_copy(peer, me_p).wait_send()
        sum1_copy(peer, me_p).wait_send()
    for peer in stream_peers:
        sum2_copy(peer, me_s).wait_send()
    for d in range(8):

        @pl.when(exists(OFFSETS[d]))
        def _(d=d):
            for k in range(ITERS + 1):
                for q in range(PARTS):
                    halo_copy(k, d, q).wait_send()


def outputs_body(pieces, *refs):
    steps = ITERS + 1
    basis_in, factors_in, outs = refs[:steps], refs[steps], refs[steps + 1 : steps + 3]
    factors, basis, made, load_sem, store_sem = refs[steps + 3 :]
    rows, width = basis.shape[1:]
    height = rows // pieces
    first = pltpu.make_async_copy(factors_in, factors, load_sem.at[pieces * steps])
    first.start()

    def load(n, i):
        at = pl.ds(n * height, height)
        return pltpu.make_async_copy(
            basis_in[i].at[at], basis.at[i, at], load_sem.at[n * steps + i]
        )

    def store(n, i):
        at = pl.ds(n * height, height)
        return pltpu.make_async_copy(made.at[i, at], outs[i].at[at], store_sem.at[n * 2 + i])

    for n in range(pieces):
        for i in range(steps):
            load(n, i).start()
    first.wait()
    rates = [jnp.broadcast_to(factors[i : i + 1, 0:1], (POLY, width)) for i in range(2 * ITERS + 1)]
    for n in range(pieces):
        for i in range(steps):
            load(n, i).wait()
        for base in range(n * height, (n + 1) * height, POLY):
            at = slice(base, base + POLY)
            vec = [basis[i, at, :] for i in range(steps)]
            made[0, at, :] = sum(rates[i] * vec[i] for i in range(ITERS))
            made[1, at, :] = sum(rates[ITERS + i] * vec[i] for i in range(steps))
        for i in range(2):
            store(n, i).start()
    for n in range(pieces):
        for i in range(2):
            store(n, i).wait()


def on_device(velocity, coefficient, coords, forces, line_id, line_gain, dest_span, owner_element):
    extent0, extent1, extent2 = coefficient.shape
    rows = extent0 * extent1
    points = coords.shape[1]
    n_stream, n_span = lax.axis_size("stream"), lax.axis_size("span")
    capacity = max(2, 2 * points // n_span)
    total_pts = n_span * capacity
    tables = constants(extent0, extent1)
    f32 = jnp.float32
    block = jax.ShapeDtypeStruct((rows, extent2), f32)
    vmem = pl.BlockSpec(memory_space=pltpu.VMEM)
    hbm = pl.BlockSpec(memory_space=pl.ANY)
    steps = ITERS + 1
    sizes = (n_stream, n_span, extent0, extent1, extent2, capacity)
    rows_fwd, rows_bwd, cols_fwd, cols_bwd, weight, column = [jnp.asarray(x) for x in tables]
    operands = [
        coords,
        forces,
        line_id.reshape(1, points),
        line_gain.reshape(1, -1),
        dest_span.reshape(1, points),
        owner_element.reshape(1, points),
        column,
        rows_fwd,
        rows_bwd,
        cols_fwd,
        cols_bwd,
        weight,
        velocity.reshape(3, rows, extent2),
        coefficient.reshape(rows, extent2),
    ]
    outs = pl.pallas_call(
        functools.partial(body, sizes),
        out_shape=(block,) * steps + (jax.ShapeDtypeStruct((8, LANES), f32),),
        in_specs=[hbm] * N_IN,
        out_specs=(hbm,) * steps + (vmem,),
        scratch_shapes=[pltpu.VMEM(x.shape, x.dtype) for x in operands]
        + [
            pltpu.VMEM((2 * rows, 4 * rows), jnp.bfloat16),
            pltpu.VMEM((rows, 6 * rows), jnp.bfloat16),
            pltpu.VMEM((3 * CHUNK, CHUNK), jnp.bfloat16),
            pltpu.VMEM((3 * CHUNK, CHUNK), jnp.bfloat16),
            pltpu.VMEM((steps, rows, extent2), f32),
            pltpu.VMEM((steps, rows, extent2), f32),
            pltpu.VMEM((rows, extent2), f32),
            pltpu.VMEM((n_span, 8, LANES), f32),
            pltpu.VMEM((n_span, 8, LANES), f32),
            pltpu.VMEM((rows, 2 * total_pts), f32),
            pltpu.VMEM((extent2, 2 * total_pts), f32),
            pltpu.VMEM((steps, 2, extent1, extent2), f32),
            pltpu.VMEM((steps, 2, extent0, extent2), f32),
            pltpu.VMEM((steps, 2, extent0, extent2), f32),
            pltpu.VMEM((steps, 4, 1, extent2), f32),
            pltpu.VMEM((steps, 4, 1, extent2), f32),
            pltpu.VMEM((n_span, 8, LANES), f32),
            pltpu.VMEM((n_stream, 8, LANES), f32),
            pltpu.SemaphoreType.DMA((N_IN,)),
            pltpu.SemaphoreType.DMA((steps,)),
            pltpu.SemaphoreType.DMA((n_span,)),
            pltpu.SemaphoreType.DMA((n_span,)),
            pltpu.SemaphoreType.DMA((steps, 8, PARTS)),
            pltpu.SemaphoreType.DMA((steps, 8, PARTS)),
            pltpu.SemaphoreType.DMA((n_span,)),
            pltpu.SemaphoreType.DMA((n_span,)),
            pltpu.SemaphoreType.DMA((n_stream,)),
            pltpu.SemaphoreType.DMA((n_stream,)),
        ],
        compiler_params=pltpu.CompilerParams(
            collective_id=0, has_side_effects=True, vmem_limit_bytes=60 * 1024 * 1024
        ),
        cost_estimate=pl.CostEstimate(
            flops=6 * 10**9, bytes_accessed=4 * 2**20, transcendentals=10**4
        ),
        name="wind_farm_step",
    )(*operands)
    pieces = 4
    pressure, residual = pl.pallas_call(
        functools.partial(outputs_body, pieces),
        out_shape=(block, block),
        in_specs=[hbm] * (steps + 1),
        out_specs=(hbm, hbm),
        scratch_shapes=[
            pltpu.VMEM((8, LANES), f32),
            pltpu.VMEM((steps, rows, extent2), f32),
            pltpu.VMEM((2, rows, extent2), f32),
            pltpu.SemaphoreType.DMA((1 + pieces * steps,)),
            pltpu.SemaphoreType.DMA((pieces * 2,)),
        ],
        compiler_params=pltpu.CompilerParams(vmem_limit_bytes=60 * 1024 * 1024),
        name="outputs",
    )(*outs)
    shape = (extent0, extent1, extent2)
    return pressure.reshape(shape), residual.reshape(shape)


def solution(mesh):
    return jax.shard_map(
        on_device,
        mesh=mesh,
        in_specs=(
            P(None, "stream", "span", None),
            P("stream", "span", None),
            P(None, ("stream", "span")),
            P(None, ("stream", "span")),
            P(("stream", "span")),
            P(),
            P(("stream", "span"), None),
            P(("stream", "span")),
        ),
        out_specs=(P("stream", "span", None), P("stream", "span", None)),
        check_vma=False,
    )
```

```python
import functools

import jax
import jax.numpy as jnp
import numpy as np
from jax import lax
from jax.experimental import pallas as pl
from jax.experimental.pallas import tpu as pltpu
from jax.sharding import PartitionSpec as P

POLY = 8
ITERS = 3
LANES = 128
CHUNK = 256
PARTS = 2
N_IN = 14

kernel_width = 0.45
gll_nodes = [
    -1.0,
    -0.8717401485096066,
    -0.5917001814331423,
    -0.2092992179024789,
    0.2092992179024789,
    0.5917001814331423,
    0.8717401485096066,
    1.0,
]
MESH = pl.DeviceIdType.MESH
OFFSETS = [(1, 0), (-1, 0), (0, 1), (0, -1), (1, 1), (1, -1), (-1, 1), (-1, -1)]


def legendre_value(point, degree):
    previous = 1.0
    current = point
    for order in range(1, degree):
        following = ((2 * order + 1) * point * current - order * previous) / (order + 1)
        previous = current
        current = following
    return current


def gll_tables():
    degree = POLY - 1
    values = [legendre_value(point, degree) for point in gll_nodes]
    weights = [2.0 / (degree * (degree + 1) * value * value) for value in values]
    diffmat = np.zeros((POLY, POLY))
    for i in range(POLY):
        for j in range(POLY):
            if i != j:
                diffmat[i, j] = values[i] / (values[j] * (gll_nodes[i] - gll_nodes[j]))
    diffmat[0, 0] = -degree * (degree + 1) / 4.0
    diffmat[-1, -1] = degree * (degree + 1) / 4.0
    return (
        np.asarray(gll_nodes, np.float32),
        np.asarray(weights, np.float32),
        np.asarray(diffmat, np.float32),
    )


def constants(extent0, extent1):
    nodes, weights, diffmat = gll_tables()
    eye = functools.partial(np.eye, dtype=np.float32)
    along0 = np.kron(eye(extent0 // POLY), np.kron(diffmat, eye(extent1)))
    along1 = np.kron(eye(extent0 * extent1 // POLY), diffmat)
    rows = np.concatenate([along0, along1], axis=0)
    cols = np.kron(eye(CHUNK // POLY), diffmat)

    row_weight = np.kron(np.tile(weights, extent0 // POLY), np.tile(weights, extent1 // POLY))
    row_weight = row_weight.astype(np.float32)
    weight = row_weight[:, None] * np.tile(weights, CHUNK // POLY)[None, :]
    table = np.concatenate([nodes[:, None], weights[:, None], diffmat.T * weights[None, :]], axis=1)
    column = np.repeat(table.T.reshape(-1, 1), LANES, axis=1)
    return rows, rows.T.copy(), cols.T.copy(), cols, weight, column


def split2(value):
    high = value.astype(jnp.bfloat16)
    low = (value - high.astype(jnp.float32)).astype(jnp.bfloat16)
    return high, low


def split3(value):
    high = value.astype(jnp.bfloat16)
    rest = value - high.astype(jnp.float32)
    middle = rest.astype(jnp.bfloat16)
    low = (rest - middle.astype(jnp.float32)).astype(jnp.bfloat16)
    return high, middle, low


def dot(first, second):
    return jnp.dot(first, second, preferred_element_type=jnp.float32)


def dot_nt(first, second):
    return lax.dot_general(
        first, second, (((1,), (1,)), ((), ())), preferred_element_type=jnp.float32
    )


def stacked(value, axis):
    high, low = split2(value)
    return jnp.concatenate([high, low, high], axis=axis)


def combine(first, second, moments, shift):
    total = 0.0
    for i, x in enumerate(first):
        for j, y in enumerate(second):
            total = total + x * y * moments[i + j + shift]
    return total


def body(sizes, *refs):
    n_stream, n_span, extent0, extent1, extent2, capacity = sizes
    n_out = ITERS + 2
    hbm_in, outs = refs[:N_IN], refs[N_IN : N_IN + n_out]
    basis_out, factors = outs[: ITERS + 1], outs[ITERS + 1]
    vmem_in = refs[N_IN + n_out : 2 * N_IN + n_out]
    (
        rows_fwd,
        rows_bwd,
        cols_fwd,
        cols_bwd,
        basis,
        work,
        joined,
        out_pts,
        in_pts,
        lhs_pts,
        rhs_pts,
        recv_stream,
        send_span,
        recv_span,
        send_edge,
        recv_edge,
        sums1,
        sums2,
        load_sem,
        store_sem,
        pts_send,
        pts_recv,
        halo_send,
        halo_recv,
        sum1_send,
        sum1_recv,
        sum2_send,
        sum2_recv,
    ) = refs[2 * N_IN + n_out :]
    (
        coords,
        forces,
        line_id,
        line_gain,
        dest_span,
        owner,
        nodes,
        rows_fwd_f32,
        rows_bwd_f32,
        cols_fwd_f32,
        cols_bwd_f32,
        weight,
        vel,
        metric,
    ) = vmem_in
    rows = extent0 * extent1
    me_s, me_p = lax.axis_index("stream"), lax.axis_index("span")

    def exists(offset):
        s, p = me_s + offset[0], me_p + offset[1]
        return (s >= 0) & (s < n_stream) & (p >= 0) & (p < n_span)

    def at_offset(offset):
        return (
            lax.rem(me_s + offset[0] + n_stream, n_stream),
            lax.rem(me_p + offset[1] + n_span, n_span),
        )

    span_peers = [lax.rem(me_p + j, n_span) for j in range(1, n_span)]
    stream_peers = [lax.rem(me_s + j, n_stream) for j in range(1, n_stream)]

    barrier = pltpu.get_barrier_semaphore()
    for peer in span_peers:
        pl.semaphore_signal(barrier, inc=1, device_id=(me_s, peer), device_id_type=MESH)
    for peer in stream_peers:
        pl.semaphore_signal(barrier, inc=1, device_id=(peer, me_p), device_id_type=MESH)
    greeted = n_span - 1 + n_stream - 1
    for offset in OFFSETS[4:]:

        @pl.when(exists(offset))
        def _(offset=offset):
            pl.semaphore_signal(
                barrier, inc=1, device_id=at_offset(offset), device_id_type=MESH
            )

        greeted = greeted + exists(offset).astype(jnp.int32)

    loads = [
        pltpu.make_async_copy(hbm_in[n], vmem_in[n], load_sem.at[n]) for n in range(N_IN)
    ]
    for load in loads:
        load.start()

    def from_offset(d):
        return exists((-OFFSETS[d][0], -OFFSETS[d][1]))

    for d in range(8):
        buffer = (recv_stream, recv_span, recv_edge)[0 if d < 2 else 1 if d < 4 else 2]
        at = d if d < 2 else d - 2 if d < 4 else d - 4

        @pl.when(jnp.logical_not(from_offset(d)))
        def _(buffer=buffer, at=at):
            for k in range(ITERS + 1):
                buffer[k, at] = jnp.zeros(buffer.shape[2:], jnp.float32)

    points = coords.shape[1]
    group = LANES // capacity
    groups = n_span // group
    lines = line_gain.shape[1]
    earlier = (
        lax.broadcasted_iota(jnp.int32, (points, points), 0)
        < lax.broadcasted_iota(jnp.int32, (points, points), 1)
    ).astype(jnp.bfloat16)
    for load in loads[:7]:
        load.wait()
    ids = line_id[...]
    chosen = (lax.broadcasted_iota(jnp.int32, (lines, points), 0) == ids).astype(jnp.bfloat16)
    gain = sum(dot(part, chosen) for part in reversed(split3(line_gain[...])))
    scaled = forces[...] * gain
    target = dest_span[...]
    spans_at = lax.broadcasted_iota(jnp.int32, (n_span, points), 0)
    named = (spans_at == target).astype(jnp.float32)
    before = dot(named.astype(jnp.bfloat16), earlier)
    rank = jnp.sum(named * before, axis=0, keepdims=True).astype(jnp.int32)
    slot = target * LANES + lax.rem(me_p, group) * capacity + rank
    payload = jnp.concatenate(
        [
            coords[...],
            scaled,
            owner[...].astype(jnp.float32),
            jnp.zeros((1, points), jnp.float32),
        ],
        axis=0,
    )
    parts = jnp.concatenate(
        [p.astype(jnp.float32) for p in split3(payload)], axis=0
    ).astype(jnp.bfloat16)
    for dest in range(n_span):
        placed = (
            lax.broadcasted_iota(jnp.int32, (LANES, points), 0) + dest * LANES == slot
        ).astype(jnp.float32).astype(jnp.bfloat16)
        tile = dot_nt(parts, placed)
        out_pts[dest] = (tile[16:24] + tile[8:16]) + tile[0:8]

    pl.semaphore_wait(barrier, greeted)

    def points_copy(peer, slot_at):
        return pltpu.make_async_remote_copy(
            src_ref=out_pts.at[peer],
            dst_ref=in_pts.at[slot_at],
            send_sem=pts_send.at[peer],
            recv_sem=pts_recv.at[slot_at],
            device_id=(me_s, peer),
            device_id_type=MESH,
        )

    for peer in span_peers:
        points_copy(peer, me_p).start()
    in_pts[me_p] = out_pts[me_p]

    for load in loads[7:12]:
        load.wait()
    high, low = split2(rows_fwd_f32[...])
    rows_fwd[...] = jnp.concatenate([high, high, low, low], axis=1)
    high, low = split2(rows_bwd_f32[...])
    rows_bwd[...] = jnp.concatenate([high, high, low], axis=1)
    for matrix, out in ((cols_fwd_f32, cols_fwd), (cols_bwd_f32, cols_bwd)):
        high, low = split2(matrix[...])
        out[...] = jnp.concatenate([high, high, low], axis=0)

    chunks = [slice(c, c + CHUNK) for c in range(0, extent2, CHUNK)]
    for load in loads[12:]:
        load.wait()
    part_width = extent2 // PARTS
    groups_at = [slice(c.start, c.stop) for c in chunks[: len(chunks) // PARTS]]
    for start in range(part_width, extent2, part_width):
        groups_at.append(slice(start, start + part_width))

    def weight_over(cols):
        return jnp.concatenate([weight[...]] * ((cols.stop - cols.start) // CHUNK), axis=1)

    def times_cols(value, matrix):
        count = value.shape[1] // CHUNK
        tall = jnp.concatenate(
            [value[:, i * CHUNK : (i + 1) * CHUNK] for i in range(count)], axis=0
        )
        tall = dot(stacked(tall, 1), matrix[...])
        return jnp.concatenate([tall[i * rows : (i + 1) * rows] for i in range(count)], axis=1)

    for start in range(0, extent2, part_width):
        cols = slice(start, start + part_width)
        w = weight_over(cols)
        both = jnp.concatenate([w * vel[0, :, cols], w * vel[1, :, cols]], axis=0)
        work[0, :, cols] = dot(rows_bwd[...], stacked(both, 0)) + times_cols(
            w * vel[2, :, cols], cols_bwd
        )
        metric[:, cols] = metric[:, cols] * w

    for peer in span_peers:
        points_copy(peer, peer).wait_recv()

    elems2 = extent2 // POLY
    total_pts = groups * LANES
    node_col = nodes[0:POLY]
    weight_col = nodes[POLY : 2 * POLY]
    diff_cols = [nodes[(2 + a) * POLY : (3 + a) * POLY] for a in range(POLY)]
    for g in range(groups):
        tile = in_pts[g * group]
        for i in range(1, group):
            tile = tile + in_pts[g * group + i]
        lanes = slice(g * LANES, (g + 1) * LANES)
        lanes_diff = slice(total_pts + g * LANES, total_pts + (g + 1) * LANES)
        plain, diff = [], []
        for k in range(3):
            kern = jnp.exp(-(((node_col - tile[k : k + 1]) / kernel_width) ** 2))
            plain.append(weight_col * kern)
            diff.append(sum(diff_cols[a] * kern[a : a + 1] for a in range(POLY)))
        elem = tile[6:7].astype(jnp.int32)
        elem_y = lax.rem(lax.div(elem, elems2), extent1 // POLY)
        elem_x = lax.div(elem, elems2 * (extent1 // POLY))
        elem_z = lax.rem(elem, elems2)
        for a in range(extent0):
            for ey in range(extent1 // POLY):
                mine = (elem_x == a // POLY) & (elem_y == ey)
                at = slice(a % POLY, a % POLY + 1)
                factor0 = jnp.where(mine, tile[3:4] * diff[0][at], 0.0)
                factor1 = jnp.where(mine, tile[4:5] * plain[0][at], 0.0)
                factor2 = jnp.where(mine, tile[5:6] * plain[0][at], 0.0)
                base = a * extent1 + ey * POLY
                lhs_pts[base : base + POLY, lanes] = factor0 * plain[1] + factor1 * diff[1]
                lhs_pts[base : base + POLY, lanes_diff] = factor2 * plain[1]
        for ez in range(elems2):
            at = slice(ez * POLY, (ez + 1) * POLY)
            rhs_pts[at, lanes] = jnp.where(elem_z == ez, plain[2], 0.0)
            rhs_pts[at, lanes_diff] = jnp.where(elem_z == ez, diff[2], 0.0)

    left_pts = stacked(lhs_pts[...], 1)

    def tile_sum(value):
        total = jnp.sum(value.reshape(rows // POLY, POLY, value.shape[1]), axis=0)
        return sum(total[:, at : at + LANES] for at in range(0, value.shape[1], LANES))

    def rhs_chunk(cols):
        high, low = split2(rhs_pts[cols, :])
        force = dot_nt(left_pts, jnp.concatenate([high, high, low], axis=1))
        work[0, :, cols] = work[0, :, cols] + force

    def operator_group(k, cols):
        field = basis[k, :, cols]
        high, low = split2(field)
        m = metric[:, cols]
        grad = dot(rows_fwd[...], jnp.concatenate([high, low, high, low], axis=0))
        grad2 = times_cols(field, cols_fwd)
        both = jnp.concatenate([grad[:rows] * m, grad[rows:] * m], axis=0)
        out = (
            dot(rows_bwd[...], stacked(both, 0))
            + times_cols(grad2 * m, cols_bwd)
            + weight_over(cols) * field
        )
        work[k + 1, :, cols] = out
        return tile_sum(field * work[k, :, cols]), tile_sum(field * out)

    last0, last1 = extent0 - 1, extent1 - 1

    def halo_copy(k, d, q):
        cols = pl.ds(q * part_width, part_width)
        if d < 2:
            src = work.at[k, pl.ds(last0 * extent1 if d == 0 else 0, extent1), cols]
            dst = recv_stream.at[k, d, :, cols]
        elif d < 4:
            src, dst = send_span.at[k, d - 2, :, cols], recv_span.at[k, d - 2, :, cols]
        else:
            src, dst = send_edge.at[k, d - 4, :, cols], recv_edge.at[k, d - 4, :, cols]
        return pltpu.make_async_remote_copy(
            src_ref=src,
            dst_ref=dst,
            send_sem=halo_send.at[k, d, q],
            recv_sem=halo_recv.at[k, d, q],
            device_id=at_offset(OFFSETS[d]),
            device_id_type=MESH,
        )

    def send_faces(k, q):
        def start(d):
            @pl.when(exists(OFFSETS[d]))
            def _():
                halo_copy(k, d, q).start()

        start(0)
        start(1)
        cols = slice(q * part_width, (q + 1) * part_width)
        for a in range(extent0):
            top = work[k, a * extent1 + last1 : a * extent1 + last1 + 1, cols]
            bottom = work[k, a * extent1 : a * extent1 + 1, cols]
            send_span[k, 0, a : a + 1, cols] = top
            send_span[k, 1, a : a + 1, cols] = bottom
            if a == last0:
                send_edge[k, 0, :, cols] = top
                send_edge[k, 1, :, cols] = bottom
            if a == 0:
                send_edge[k, 2, :, cols] = top
                send_edge[k, 3, :, cols] = bottom
        for d in range(2, 8):
            start(d)

    def join(k, q):
        for d in (2, 3, 4, 5, 6, 7, 0, 1):

            @pl.when(from_offset(d))
            def _(d=d):
                halo_copy(k, d, q).wait_recv()

        cols = slice(q * part_width, (q + 1) * part_width)
        sub = lax.broadcasted_iota(jnp.int32, (POLY, part_width), 0)
        for a in range(extent0):
            tiles = []
            for ey in range(extent1 // POLY):
                base = a * extent1 + ey * POLY
                x = work[k, base : base + POLY, cols]
                if a == 0:
                    x = x + recv_stream[k, 0, ey * POLY : (ey + 1) * POLY, cols]
                if a == last0:
                    x = x + recv_stream[k, 1, ey * POLY : (ey + 1) * POLY, cols]
                tiles.append(x)
            lower = recv_span[k, 0, a : a + 1, cols]
            upper = recv_span[k, 1, a : a + 1, cols]
            if a == 0:
                lower = lower + recv_edge[k, 0, :, cols]
                upper = upper + recv_edge[k, 1, :, cols]
            if a == last0:
                lower = lower + recv_edge[k, 2, :, cols]
                upper = upper + recv_edge[k, 3, :, cols]
            for ey, x in enumerate(tiles):
                below = lower if ey == 0 else pltpu.roll(tiles[ey - 1], 1, 0)
                above = upper if ey + 1 == len(tiles) else pltpu.roll(tiles[ey + 1], POLY - 1, 0)
                base = a * extent1 + ey * POLY
                joined[base : base + POLY, cols] = (
                    x + jnp.where(sub == 0, below, 0.0) + jnp.where(sub == POLY - 1, above, 0.0)
                )

    def assemble(k, cols):
        start, stop = max(cols.start - LANES, 0), min(cols.stop + LANES, extent2)
        width = stop - start
        lane = lax.broadcasted_iota(jnp.int32, (POLY, CHUNK), 1) + cols.start
        first2 = (lane % POLY == 0) & (lane > 0)
        last2 = (lane % POLY == POLY - 1) & (lane < extent2 - 1)
        inner = slice(cols.start - start, cols.stop - start)
        for base in range(0, rows, POLY):
            x = joined[base : base + POLY, start:stop]
            lower = pltpu.roll(x, 1, 1)[:, inner]
            upper = pltpu.roll(x, width - 1, 1)[:, inner]
            basis[k, base : base + POLY, cols] = (
                x[:, inner] + jnp.where(first2, lower, 0.0) + jnp.where(last2, upper, 0.0)
            )

    def store(k):
        return pltpu.make_async_copy(basis.at[k], basis_out[k], store_sem.at[k])

    def joined_groups(k):
        have = 0
        for cols in groups_at:
            need = min(cols.stop // part_width + 1, PARTS)
            while have < need:
                join(k, have)
                have += 1
            for start in range(cols.start, cols.stop, CHUNK):
                assemble(k, slice(start, start + CHUNK))
            if cols.stop == extent2:
                store(k).start()
            yield cols

    for cols in chunks:
        rhs_chunk(cols)
        if cols.stop % part_width == 0:
            send_faces(0, cols.stop // part_width - 1)
    mine = []
    for k in range(ITERS):
        even = odd = 0.0
        for cols in joined_groups(k):
            more = operator_group(k, cols)
            even, odd = even + more[0], odd + more[1]
            if cols.stop % part_width == 0:
                send_faces(k + 1, cols.stop // part_width - 1)
        mine += [even, odd]

    mine = [jnp.sum(total, axis=0, keepdims=True) for total in mine]
    mine.append(jnp.zeros((8 - len(mine), LANES), jnp.float32))
    sums1[me_p] = jnp.concatenate(mine, axis=0)

    def sum1_copy(peer, slot_at):
        return pltpu.make_async_remote_copy(
            src_ref=sums1.at[me_p],
            dst_ref=sums1.at[slot_at],
            send_sem=sum1_send.at[peer],
            recv_sem=sum1_recv.at[slot_at],
            device_id=(me_s, peer),
            device_id_type=MESH,
        )

    def sum2_copy(peer, slot_at):
        return pltpu.make_async_remote_copy(
            src_ref=sums2.at[me_s],
            dst_ref=sums2.at[slot_at],
            send_sem=sum2_send.at[peer],
            recv_sem=sum2_recv.at[slot_at],
            device_id=(peer, me_p),
            device_id_type=MESH,
        )

    for peer in span_peers:
        sum1_copy(peer, me_p).start()
    for peer in span_peers:
        sum1_copy(peer, peer).wait_recv()
    total = sums1[0]
    for i in range(1, n_span):
        total = total + sums1[i]
    sums2[me_s] = total
    for peer in stream_peers:
        sum2_copy(peer, me_s).start()
    for _ in joined_groups(ITERS):
        pass
    for peer in stream_peers:
        sum2_copy(peer, peer).wait_recv()
    total = sums2[0]
    for i in range(1, n_stream):
        total = total + sums2[i]
    total = jnp.broadcast_to(jnp.sum(total, axis=1, keepdims=True), (8, LANES))
    moments = [total[n : n + 1] for n in range(2 * ITERS)]

    one = jnp.ones((1, LANES), jnp.float32)
    res, direction, pres = [one], [one], [0.0] * ITERS
    norm = moments[0]
    for iteration in range(ITERS):
        step_len = norm / combine(direction, direction, moments, 1)
        for i, x in enumerate(direction):
            pres[i] = pres[i] + step_len * x
        res = res + [0.0]
        res = [res[0]] + [x - step_len * y for x, y in zip(res[1:], direction)]
        if iteration + 1 < ITERS:
            norm_next = combine(res, res, moments, 0)
            ratio = norm_next / norm
            direction = [x + ratio * y for x, y in zip(res, direction + [0.0])]
            norm = norm_next

    factors[...] = jnp.concatenate(pres + res + [jnp.zeros((1, LANES), jnp.float32)], axis=0)

    for k in range(ITERS + 1):
        store(k).wait()
    for peer in span_peers:
        points_copy(peer, me_p).wait_send()
        sum1_copy(peer, me_p).wait_send()
    for peer in stream_peers:
        sum2_copy(peer, me_s).wait_send()
    for d in range(8):

        @pl.when(exists(OFFSETS[d]))
        def _(d=d):
            for k in range(ITERS + 1):
                for q in range(PARTS):
                    halo_copy(k, d, q).wait_send()


def outputs_body(pieces, *refs):
    steps = ITERS + 1
    basis_in, factors_in, outs = refs[:steps], refs[steps], refs[steps + 1 : steps + 3]
    factors, basis, made, load_sem, store_sem = refs[steps + 3 :]
    rows, width = basis.shape[1:]
    height = rows // pieces
    first = pltpu.make_async_copy(factors_in, factors, load_sem.at[pieces * steps])
    first.start()

    def load(n, i):
        at = pl.ds(n * height, height)
        return pltpu.make_async_copy(
            basis_in[i].at[at], basis.at[i, at], load_sem.at[n * steps + i]
        )

    def store(n, i):
        at = pl.ds(n * height, height)
        return pltpu.make_async_copy(made.at[i, at], outs[i].at[at], store_sem.at[n * 2 + i])

    for n in range(pieces):
        for i in range(steps):
            load(n, i).start()
    first.wait()
    rates = [jnp.broadcast_to(factors[i : i + 1, 0:1], (POLY, width)) for i in range(2 * ITERS + 1)]
    for n in range(pieces):
        for i in range(steps):
            load(n, i).wait()
        for base in range(n * height, (n + 1) * height, POLY):
            at = slice(base, base + POLY)
            vec = [basis[i, at, :] for i in range(steps)]
            made[0, at, :] = sum(rates[i] * vec[i] for i in range(ITERS))
            made[1, at, :] = sum(rates[ITERS + i] * vec[i] for i in range(steps))
        for i in range(2):
            store(n, i).start()
    for n in range(pieces):
        for i in range(2):
            store(n, i).wait()


def on_device(velocity, coefficient, coords, forces, line_id, line_gain, dest_span, owner_element):
    extent0, extent1, extent2 = coefficient.shape
    rows = extent0 * extent1
    points = coords.shape[1]
    n_stream, n_span = lax.axis_size("stream"), lax.axis_size("span")
    capacity = max(2, 2 * points // n_span)
    total_pts = n_span * capacity
    tables = constants(extent0, extent1)
    f32 = jnp.float32
    block = jax.ShapeDtypeStruct((rows, extent2), f32)
    vmem = pl.BlockSpec(memory_space=pltpu.VMEM)
    hbm = pl.BlockSpec(memory_space=pl.ANY)
    steps = ITERS + 1
    sizes = (n_stream, n_span, extent0, extent1, extent2, capacity)
    rows_fwd, rows_bwd, cols_fwd, cols_bwd, weight, column = [jnp.asarray(x) for x in tables]
    operands = [
        coords,
        forces,
        line_id.reshape(1, points),
        line_gain.reshape(1, -1),
        dest_span.reshape(1, points),
        owner_element.reshape(1, points),
        column,
        rows_fwd,
        rows_bwd,
        cols_fwd,
        cols_bwd,
        weight,
        velocity.reshape(3, rows, extent2),
        coefficient.reshape(rows, extent2),
    ]
    outs = pl.pallas_call(
        functools.partial(body, sizes),
        out_shape=(block,) * steps + (jax.ShapeDtypeStruct((8, LANES), f32),),
        in_specs=[hbm] * N_IN,
        out_specs=(hbm,) * steps + (vmem,),
        scratch_shapes=[pltpu.VMEM(x.shape, x.dtype) for x in operands]
        + [
            pltpu.VMEM((2 * rows, 4 * rows), jnp.bfloat16),
            pltpu.VMEM((rows, 6 * rows), jnp.bfloat16),
            pltpu.VMEM((3 * CHUNK, CHUNK), jnp.bfloat16),
            pltpu.VMEM((3 * CHUNK, CHUNK), jnp.bfloat16),
            pltpu.VMEM((steps, rows, extent2), f32),
            pltpu.VMEM((steps, rows, extent2), f32),
            pltpu.VMEM((rows, extent2), f32),
            pltpu.VMEM((n_span, 8, LANES), f32),
            pltpu.VMEM((n_span, 8, LANES), f32),
            pltpu.VMEM((rows, 2 * total_pts), f32),
            pltpu.VMEM((extent2, 2 * total_pts), f32),
            pltpu.VMEM((steps, 2, extent1, extent2), f32),
            pltpu.VMEM((steps, 2, extent0, extent2), f32),
            pltpu.VMEM((steps, 2, extent0, extent2), f32),
            pltpu.VMEM((steps, 4, 1, extent2), f32),
            pltpu.VMEM((steps, 4, 1, extent2), f32),
            pltpu.VMEM((n_span, 8, LANES), f32),
            pltpu.VMEM((n_stream, 8, LANES), f32),
            pltpu.SemaphoreType.DMA((N_IN,)),
            pltpu.SemaphoreType.DMA((steps,)),
            pltpu.SemaphoreType.DMA((n_span,)),
            pltpu.SemaphoreType.DMA((n_span,)),
            pltpu.SemaphoreType.DMA((steps, 8, PARTS)),
            pltpu.SemaphoreType.DMA((steps, 8, PARTS)),
            pltpu.SemaphoreType.DMA((n_span,)),
            pltpu.SemaphoreType.DMA((n_span,)),
            pltpu.SemaphoreType.DMA((n_stream,)),
            pltpu.SemaphoreType.DMA((n_stream,)),
        ],
        compiler_params=pltpu.CompilerParams(
            collective_id=0, has_side_effects=True, vmem_limit_bytes=60 * 1024 * 1024
        ),
        cost_estimate=pl.CostEstimate(
            flops=6 * 10**9, bytes_accessed=4 * 2**20, transcendentals=10**4
        ),
        name="wind_farm_step",
    )(*operands)
    pieces = 4
    pressure, residual = pl.pallas_call(
        functools.partial(outputs_body, pieces),
        out_shape=(block, block),
        in_specs=[hbm] * (steps + 1),
        out_specs=(hbm, hbm),
        scratch_shapes=[
            pltpu.VMEM((8, LANES), f32),
            pltpu.VMEM((steps, rows, extent2), f32),
            pltpu.VMEM((2, rows, extent2), f32),
            pltpu.SemaphoreType.DMA((1 + pieces * steps,)),
            pltpu.SemaphoreType.DMA((pieces * 2,)),
        ],
        compiler_params=pltpu.CompilerParams(vmem_limit_bytes=60 * 1024 * 1024),
        name="outputs",
    )(*outs)
    shape = (extent0, extent1, extent2)
    return pressure.reshape(shape), residual.reshape(shape)


def solution(mesh):
    return jax.shard_map(
        on_device,
        mesh=mesh,
        in_specs=(
            P(None, "stream", "span", None),
            P("stream", "span", None),
            P(None, ("stream", "span")),
            P(None, ("stream", "span")),
            P(("stream", "span")),
            P(),
            P(("stream", "span"), None),
            P(("stream", "span")),
        ),
        out_specs=(P("stream", "span", None), P("stream", "span", None)),
        check_vma=False,
    )
```
